256 devices in a mesh: dp: 4 (over x), group: 2 (over core), expert: 32 (over y, z).
Axes of the slice: x: 4, y: 4, z: 8, core: 2. Of those that a mesh axis runs over, the one named last changes fastest.
Arguments:
- tokens: bfloat16 [8192, 3584], P(('group', 'expert')), may hold values from -6 to 6
- expert_ids: int32 [8192, 2], P(('group', 'expert')), may hold values from 0 to 31, all different within a row; in each aligned block of 128 rows (0 to 127, 128 to 255, ...) at most 10 rows name the same one
- gates: float32 [8192, 2], P(('group', 'expert')), may hold values from 0.1 to 1
- w_gate: bfloat16 [32, 3584, 3072], P('expert', None, ('dp', 'group')), may hold values from -0.09375 to 0.09375
- w_up: bfloat16 [32, 3584, 3072], P('expert', None, ('dp', 'group')), may hold values from -0.09375 to 0.09375
- w_down: bfloat16 [32, 3072, 3584], P('expert', ('dp', 'group')), may hold values from -0.109375 to 0.109375
- cotangent: bfloat16 [8192, 3584], P(('group', 'expert'), 'dp'), may hold values from -1.1953125 to 1.1953125
Outputs:
- mixed: bfloat16 [8192, 3584], P(('group', 'expert'), 'dp')
- d_tokens: bfloat16 [8192, 3584], P(('group', 'expert'), 'dp')
- d_gates: float32 [8192, 2], P(('group', 'expert'))
The draws below stay inside these ranges and needn't reach their ends.
Inputs may be any that keep to these rules, and one draw needn't show every extreme that they name: `expert_ids`: the two experts of a token differ. Within each aligned block of 128 tokens no expert is named by more than 10 tokens, a bound that some block reaches.
All inputs are finite; a program needn't handle non-finite values.
Results may differ from the reference program's by a relative error of at most 0.012.
Values may be sent and summed in bfloat16 or wider, within the bound.
No kernel may reach another device: no remote copies, remote signals or barrier semaphores. Data moves between devices by JAX's collectives and lax.ppermute only.
A program may use at most 128 MiB of HBM per device.

```python
import math
import jax
import jax.numpy as jnp
import numpy as np
from jax import lax

D = 3584
HID = 3072
TOK_DEV = 128
EXPERTS = 32
CAP = 10
TOKENS = 8192
N_DP = 4
N_GROUP = 2


def level_of(rng, shape, pieces, least, largest):
    factor_of, own = 1.0, jax.random.fold_in(rng, 6)
    for dim, shards_of in pieces:
        steps = jnp.exp(jax.random.uniform(jax.random.fold_in(own, dim), (shards_of,), jnp.float32, least / len(pieces), largest / len(pieces)))
        factor_of = factor_of * jnp.repeat(steps, shape[dim] // shards_of).reshape([-1 if axis == dim else 1 for axis in range(len(shape))])
    return factor_of


def deal_out(key, own, number, rows, number_of, top, limit, slope):
    sequence = jax.random.permutation(key, number_of)
    crowded, ordinary = shares(number_of, rows * top, limit, slope, True), shares(number_of, rows * top, limit, slope, False)
    places = jnp.arange(number_of)

    def named(lengths, offset_by):
        used = int((lengths > 0).sum())
        fixed = max(1, used // 4)
        passed = fixed + (places - fixed + offset_by * (used - fixed)) % max(1, number_of - fixed)
        return jnp.zeros((number_of,), jnp.int32).at[sequence[jnp.where(places < fixed, places, passed)]].set(jnp.asarray(lengths, jnp.int32))

    lengths = jnp.where(number % 4 == 0, named(crowded, number // 4), named(ordinary, number - number // 4 - 1))
    mixed = jax.random.permutation(jax.random.fold_in(own, 3), number_of)
    giver, taker = mixed[0:number_of // 2 * 2:2], mixed[1:number_of // 2 * 2:2]
    room = jnp.minimum(lengths[giver] - 1, limit - lengths[taker]) // 2
    room = jnp.where((giver == sequence[0]) | (taker == sequence[0]) | (lengths[taker] == 0), 0, jnp.maximum(room, 0))
    passed = jax.random.randint(jax.random.fold_in(own, 4), (number_of // 2,), 0, 1 << 20) % (room + 1)
    lengths = lengths.at[giver].add(-passed).at[taker].add(passed)
    labels = jnp.searchsorted(jnp.cumsum(lengths), jnp.arange(rows * top), side="right").astype(jnp.int32)
    listing = labels.reshape(top, rows).T
    listing = listing[jax.random.permutation(jax.random.fold_in(own, 1), rows)]
    offset_by = jax.random.randint(jax.random.fold_in(own, 2), (rows, 1), 0, top)
    return jnp.take_along_axis(listing, (jnp.arange(top)[None, :] + offset_by) % top, axis=1)


def shares(number_of, total, most, skew, full):
    weights = [(1 << 20) // math.isqrt(standing ** skew) + 1 for standing in range(1, number_of + 1)]
    largest = most if full else min(most, max(-(-total // number_of), total * weights[0] // sum(weights)))
    least = 1 if total - largest >= number_of - 1 else 0
    holding, surplus = [largest] + [least] * (number_of - 1), total - largest - least * (number_of - 1)
    while surplus > 0:
        movable = [i for i in range(1, number_of) if holding[i] < largest] or [i for i in range(1, number_of) if holding[i] < most]
        whole, left = sum([weights[i] for i in movable]), surplus
        for i in movable:
            addition = min(most - holding[i], max(1, left * weights[i] // whole), surplus)
            holding[i] = holding[i] + addition
            surplus = surplus - addition
    return np.array(holding)


def normal_values(own_key, dims, scale, most, cuts=(), kind=jnp.bfloat16):
    drawn = scale * jax.random.normal(own_key, dims, jnp.float32)
    if cuts:
        drawn = drawn * level_of(own_key, dims, cuts, -0.22, 0.18)
    return jnp.clip(drawn, -most, most).astype(kind)


def setup_inputs(seed: int = 0) -> dict:
    key_list = jax.random.split(jax.random.key(seed), 8)
    tokens = normal_values(key_list[0], (TOKENS, D), 1.0, 6.0, ((0, 64),))
    expert_ids_keys = jax.random.split(jax.random.fold_in(key_list[1], 1), TOKENS // TOK_DEV)
    expert_ids_turns = jax.random.permutation(jax.random.fold_in(key_list[1], 3), TOKENS // TOK_DEV)
    expert_ids = jax.vmap(lambda own, number: deal_out(jax.random.fold_in(key_list[1], 2), own, number, TOK_DEV, EXPERTS, 2, CAP, 2))(expert_ids_keys, expert_ids_turns).reshape((TOKENS, 2))
    gates = jnp.clip(0.1 + 0.9 * jax.random.uniform(key_list[2], (TOKENS, 2), jnp.float32) ** level_of(key_list[2], (TOKENS, 2), ((0, 64),), -0.2, 0.2), 0.1, 1.0)
    w_gate = normal_values(key_list[3], (EXPERTS, D, HID), D ** -0.5, 0.09375, ((0, 32), (2, 8)))
    w_up = normal_values(key_list[4], (EXPERTS, D, HID), D ** -0.5, 0.09375, ((0, 32), (2, 8)))
    w_down = normal_values(key_list[5], (EXPERTS, HID, D), HID ** -0.5, 0.109375, ((0, 32), (1, 8)))
    cotangent = normal_values(key_list[6], (TOKENS, D), 0.2, 1.1953125, ((0, 64), (1, 4)))
    return {"tokens": tokens, "expert_ids": expert_ids, "gates": gates, "w_gate": w_gate, "w_up": w_up, "w_down": w_down, "cotangent": cotangent}


def split_sum(left, right, width, parts):
    total = jnp.zeros((left.shape[0], right.shape[1]), jnp.float32)
    for index in range(parts):
        piece = jnp.dot(left[:, index * width:(index + 1) * width], right[index * width:(index + 1) * width], preferred_element_type=jnp.float32)
        piece = lax.optimization_barrier(piece.astype(jnp.bfloat16))
        total = total + piece.astype(jnp.float32)
    return total


def split_pair(first, second, first_w, second_w, width, parts):
    total = jnp.zeros((first.shape[0], first_w.shape[0]), jnp.float32)
    for index in range(parts):
        lower = index * width
        upper = (index + 1) * width
        piece = jnp.dot(first[:, lower:upper], first_w[:, lower:upper].T, preferred_element_type=jnp.float32)
        piece = piece + jnp.dot(second[:, lower:upper], second_w[:, lower:upper].T, preferred_element_type=jnp.float32)
        piece = lax.optimization_barrier(piece.astype(jnp.bfloat16))
        total = total + piece.astype(jnp.float32)
    return total


def reference(tokens, expert_ids, gates, w_gate, w_up, w_down, cotangent):
    blocks = TOKENS // TOK_DEV
    pairs = 2 * TOK_DEV
    parts = N_DP * N_GROUP
    eighth = HID // parts
    ids = expert_ids.reshape(blocks, pairs).astype(jnp.int32)
    onehot = (ids[:, :, None] == jnp.arange(EXPERTS, dtype=jnp.int32)[None, None, :]).astype(jnp.int32)
    earlier = jnp.cumsum(onehot, axis=1) - onehot
    slot = jnp.sum(earlier * onehot, axis=2).astype(jnp.int32)
    block_of = jnp.broadcast_to(jnp.arange(blocks, dtype=jnp.int32)[:, None], (blocks, pairs))
    rows = jnp.repeat(tokens, 2, axis=0).reshape(blocks, pairs, D)
    scaled = gates.reshape(-1)[:, None] * jnp.repeat(cotangent, 2, axis=0).astype(jnp.float32)
    scaled = scaled.astype(jnp.bfloat16).reshape(blocks, pairs, D)
    xbuf = jnp.zeros((EXPERTS, blocks, CAP, D), jnp.bfloat16).at[ids, block_of, slot].set(rows)
    zbuf = jnp.zeros((EXPERTS, blocks, CAP, D), jnp.bfloat16).at[ids, block_of, slot].set(scaled)

    def serve(operands):
        xs, zs, gate_w, up_w, down_w = operands
        xrows = xs.reshape(-1, D)
        zrows = zs.reshape(-1, D)
        gate_pre = jnp.dot(xrows, gate_w, preferred_element_type=jnp.float32)
        up_pre = jnp.dot(xrows, up_w, preferred_element_type=jnp.float32)
        sigma = jax.nn.sigmoid(gate_pre)
        hidden = (gate_pre * sigma * up_pre).astype(jnp.bfloat16)
        output = split_sum(hidden, down_w, eighth, parts)
        grad_h = jnp.dot(zrows, down_w.T, preferred_element_type=jnp.float32)
        d_gate = (grad_h * up_pre * sigma * (1.0 + gate_pre * (1.0 - sigma))).astype(jnp.bfloat16)
        d_up = (grad_h * gate_pre * sigma).astype(jnp.bfloat16)
        dinput = split_pair(d_gate, d_up, gate_w, up_w, eighth, parts)
        return output, dinput

    outs, dxs = lax.map(serve, (xbuf, zbuf, w_gate, w_up, w_down))
    outs = outs.reshape(EXPERTS, blocks, CAP, D)[ids, block_of, slot].reshape(TOKENS, 2, D)
    dxs = dxs.reshape(EXPERTS, blocks, CAP, D)[ids, block_of, slot].reshape(TOKENS, 2, D)
    mixed = jnp.sum(gates[:, :, None] * outs, axis=1).astype(jnp.bfloat16)
    d_tokens = jnp.sum(dxs, axis=1).astype(jnp.bfloat16)
    d_gates = jnp.sum(cotangent.astype(jnp.float32)[:, None, :] * outs, axis=2)
    return mixed, d_tokens, d_gates
```

```python
import functools
import jax
import jax.numpy as jnp
from jax import lax
from jax.experimental import pallas as pl
from jax.experimental.pallas import tpu as pltpu
from jax.sharding import PartitionSpec as P

BF = jnp.bfloat16
F32 = jnp.float32
TOK = 128
EXP = 32
MAIN = 8
OVER = 2
LANE = 128
NDP = 4
D = 3584
QD = D // NDP
CH = QD // LANE
ROWS = EXP * MAIN
WIDE = QD + OVER * LANE
ALL = ROWS + EXP * OVER
HALF = ROWS // 2
HD = 384
VMEM = 48 * 1024 * 1024
NT = (((1,), (1,)), ((), ()))
TN = (((0,), (0,)), ((), ()))


def params():
    return pltpu.CompilerParams(vmem_limit_bytes=VMEM)


def iota(shape, dim):
    return lax.broadcasted_iota(jnp.int32, shape, dim)


def dot(a, b, dims=(((1,), (0,)), ((), ()))):
    return lax.dot_general(a, b, dims, preferred_element_type=F32)


def spread():
    row, col = iota((ROWS, CH * EXP), 0), iota((ROWS, CH * EXP), 1)
    return ((row % MAIN == col // EXP) & (row // MAIN == col % EXP)).astype(F32).astype(BF)


def pack(over):
    parts = [
        jnp.concatenate([over[c * EXP:(c + 1) * EXP, r * LANE:(r + 1) * LANE] for c in range(OVER)], axis=1)
        for r in range(CH)
    ]
    return dot(spread(), jnp.concatenate(parts, axis=0)).astype(BF)


def unpack(packed):
    rows = dot(spread(), packed, TN).astype(BF)
    parts = [
        jnp.concatenate([rows[r * EXP:(r + 1) * EXP, c * LANE:(c + 1) * LANE] for c in range(OVER)], axis=0)
        for r in range(CH)
    ]
    return jnp.concatenate(parts, axis=1)


def join(piece):
    return jnp.concatenate([piece[:, :QD], unpack(piece[:, QD:])], axis=0)


def split(rows):
    return jnp.concatenate([rows[:ROWS], pack(rows[ROWS:])], axis=1)


def choose(ids):
    lane = iota((TOK, EXP), 1)
    hot = [(ids[:, k:k + 1] == lane).astype(F32) for k in range(2)]
    both = hot[0] + hot[1]
    lower = (iota((TOK, TOK), 1) < iota((TOK, TOK), 0)).astype(F32).astype(BF)
    earlier = dot(lower, both.astype(BF))
    out = []
    for k in range(2):
        slot = jnp.sum(earlier * hot[k], axis=1, keepdims=True).astype(jnp.int32)
        e = ids[:, k:k + 1]
        dest = jnp.where(slot < MAIN, e * MAIN + slot, ROWS + (slot - MAIN) * EXP + e)
        out.append((iota((TOK, ALL), 1) == dest).astype(F32).astype(BF))
    return out


def pack_kernel(d_ref, ids_ref, gates_ref, tok_ref, cot_ref, x_ref, z_ref):
    m0, m1 = choose(ids_ref[...])
    gates = gates_ref[...]
    cot = cot_ref[...].astype(F32)
    x_ref[...] = split(dot(m0 + m1, tok_ref[...], TN).astype(BF))
    z0 = (gates[:, 0:1] * cot).astype(BF)
    z1 = (gates[:, 1:2] * cot).astype(BF)
    z_ref[...] = split((dot(m0, z0, TN) + dot(m1, z1, TN)).astype(BF))


def pack_call(d, ids, gates, tokens, cot):
    full = lambda shape: pl.BlockSpec(shape, lambda i, d_ref: (0, 0))
    shape = jax.ShapeDtypeStruct((ROWS, WIDE), BF)
    return pl.pallas_call(
        pack_kernel,
        grid_spec=pltpu.PrefetchScalarGridSpec(
            num_scalar_prefetch=1,
            grid=(1,),
            in_specs=[
                full((TOK, 2)),
                full((TOK, 2)),
                pl.BlockSpec((TOK, QD), lambda i, d_ref: (0, d_ref[0])),
                full((TOK, QD)),
            ],
            out_specs=[full((ROWS, WIDE))] * 2,
        ),
        out_shape=[shape, shape],
        compiler_params=params(),
        cost_estimate=pl.CostEstimate(flops=400_000_000, bytes_accessed=2_000_000, transcendentals=0),
    )(d, ids, gates, tokens, cot)


def pieces_of(refs):
    p0, p1, p2a, p2b, p3 = refs
    return [
        lambda: p0[...],
        lambda: p1[...],
        lambda: jnp.concatenate([p2a[...], p2b[...]], axis=0),
        lambda: p3[...],
    ]


def store_piece(refs, j, value):
    p0, p1, p2a, p2b, p3 = refs
    if j == 2:
        p2a[...] = value[:HALF]
        p2b[...] = value[HALF:]
    else:
        (p0, p1, None, p3)[j][...] = value


def fwd_kernel(d_ref, *refs):
    xs, (wg0, wg1, wu0, wu1, wd0, wd1), outs = refs[:5], refs[5:11], refs[11:16]
    a_ref, b_ref, h_ref = refs[16:]
    step = pl.program_id(0)
    for j, piece in enumerate(pieces_of(xs)):
        @pl.when(step == j)
        def _(j=j, piece=piece):
            rows = join(piece())
            for ref, pair in ((a_ref, (wg0, wg1)), (b_ref, (wu0, wu1))):
                for c, w in enumerate(pair):
                    part = dot(rows, w[...])
                    at = (slice(None), pl.ds(c * HD, HD))
                    ref[at] = part if j == 0 else ref[at] + part

    @pl.when(step == NDP - 1)
    def _():
        a, b = a_ref[...], b_ref[...]
        h_ref[...] = (a * jax.nn.sigmoid(a) * b).astype(BF)

    for j in range(NDP):
        @pl.when(step == NDP + j)
        def _(j=j):
            out = dot(h_ref[:, :HD], wd0[...]) + dot(h_ref[:, HD:], wd1[...])
            store_piece(outs, j, split(out.astype(BF)))


def bwd_kernel(d_ref, *refs):
    zs, (a_ref, b_ref), (wg0, wg1, wu0, wu1, wd0, wd1), outs = refs[:5], refs[5:7], refs[7:13], refs[13:18]
    g_ref, da_ref, db_ref = refs[18:]
    step = pl.program_id(0)
    for j, piece in enumerate(pieces_of(zs)):
        @pl.when(step == j)
        def _(j=j, piece=piece):
            rows = join(piece())
            for c, w in enumerate((wd0, wd1)):
                part = dot(rows, w[...], NT)
                at = (slice(None), pl.ds(c * HD, HD))
                g_ref[at] = part if j == 0 else g_ref[at] + part

    @pl.when(step == NDP - 1)
    def _():
        g, a, b = g_ref[...], a_ref[...], b_ref[...]
        s = jax.nn.sigmoid(a)
        da_ref[...] = (g * b * s * (1.0 + a * (1.0 - s))).astype(BF)
        db_ref[...] = (g * a * s).astype(BF)

    for j in range(NDP):
        @pl.when(step == NDP + j)
        def _(j=j):
            dx = dot(da_ref[:, :HD], wg0[...], NT) + dot(da_ref[:, HD:], wg1[...], NT)
            dx = dx + dot(db_ref[:, :HD], wu0[...], NT) + dot(db_ref[:, HD:], wu1[...], NT)
            store_piece(outs, j, split(dx.astype(BF)))


def whole(shape):
    return pl.BlockSpec(shape, lambda i, d_ref: (0, 0))


def first(i, d_ref):
    return (d_ref[0] + jnp.minimum(i, NDP - 1)) % NDP


def second(i, d_ref):
    return (d_ref[0] + jnp.maximum(i - NDP, 0)) % NDP


PIECES = [(ROWS, WIDE), (ROWS, WIDE), (HALF, WIDE), (HALF, WIDE), (ROWS, WIDE)]


def fwd_call(d, xs, wg, wu, wd):
    in_w = pl.BlockSpec((QD, HD), lambda i, d_ref: (first(i, d_ref), 0))
    down_w = pl.BlockSpec((HD, QD), lambda i, d_ref: (0, second(i, d_ref)))
    hidden = (ALL, 2 * HD)
    return pl.pallas_call(
        fwd_kernel,
        grid_spec=pltpu.PrefetchScalarGridSpec(
            num_scalar_prefetch=1,
            grid=(2 * NDP,),
            in_specs=[whole(s) for s in PIECES] + [in_w] * 4 + [down_w] * 2,
            out_specs=[whole(s) for s in PIECES] + [whole(hidden)] * 2,
            scratch_shapes=[pltpu.VMEM(hidden, BF)],
        ),
        out_shape=[jax.ShapeDtypeStruct(s, BF) for s in PIECES] + [jax.ShapeDtypeStruct(hidden, F32)] * 2,
        compiler_params=params(),
        cost_estimate=pl.CostEstimate(flops=5_300_000_000, bytes_accessed=22_000_000, transcendentals=300_000),
    )(d, *xs, *wg, *wu, *wd)


def bwd_call(d, zs, a, b, wg, wu, wd):
    in_w = pl.BlockSpec((QD, HD), lambda i, d_ref: (second(i, d_ref), 0))
    down_w = pl.BlockSpec((HD, QD), lambda i, d_ref: (0, first(i, d_ref)))
    hidden = (ALL, 2 * HD)
    return pl.pallas_call(
        bwd_kernel,
        grid_spec=pltpu.PrefetchScalarGridSpec(
            num_scalar_prefetch=1,
            grid=(2 * NDP,),
            in_specs=[whole(s) for s in PIECES] + [whole(hidden)] * 2 + [in_w] * 4 + [down_w] * 2,
            out_specs=[whole(s) for s in PIECES],
            scratch_shapes=[pltpu.VMEM(hidden, F32), pltpu.VMEM(hidden, BF), pltpu.VMEM(hidden, BF)],
        ),
        out_shape=[jax.ShapeDtypeStruct(s, BF) for s in PIECES],
        compiler_params=params(),
        cost_estimate=pl.CostEstimate(flops=5_300_000_000, bytes_accessed=23_000_000, transcendentals=300_000),
    )(d, *zs, a, b, *wg, *wu, *wd)


def mix_kernel(ids_ref, gates_ref, cot_ref, out_ref, mixed_ref, dg_ref):
    hots = choose(ids_ref[...])
    rows = join(out_ref[...])
    gates = gates_ref[...]
    cot = cot_ref[...].astype(F32)
    mixed = jnp.zeros((TOK, QD), F32)
    for k in range(2):
        mine = dot(hots[k], rows)
        mixed = mixed + gates[:, k:k + 1] * mine
        dg_ref[:, k:k + 1] = jnp.sum(cot * mine, axis=1, keepdims=True)
    mixed_ref[...] = mixed.astype(BF)


def mix_call(ids, gates, cot, out):
    return pl.pallas_call(
        mix_kernel,
        out_shape=[jax.ShapeDtypeStruct((TOK, QD), BF), jax.ShapeDtypeStruct((TOK, 2), F32)],
        compiler_params=params(),
        cost_estimate=pl.CostEstimate(flops=200_000_000, bytes_accessed=1_500_000, transcendentals=0),
    )(ids, gates, cot, out)


def dtok_kernel(ids_ref, dx_ref, out_ref):
    m0, m1 = choose(ids_ref[...])
    out_ref[...] = dot(m0 + m1, join(dx_ref[...])).astype(BF)


def dtok_call(ids, dx):
    return pl.pallas_call(
        dtok_kernel,
        out_shape=jax.ShapeDtypeStruct((TOK, QD), BF),
        compiler_params=params(),
        cost_estimate=pl.CostEstimate(flops=200_000_000, bytes_accessed=1_000_000, transcendentals=0),
    )(ids, dx)


def move(x, by):
    return lax.ppermute(x, "dp", [(i, (i + by) % NDP) for i in range(NDP)])


def gather_dp(own):
    low = move(own, 1)
    high = move(own, -1)
    far_a = move(low[:HALF], 1)
    far_b = move(high[HALF:], -1)
    return own, high, far_a, far_b, low


def reduce_dp(pieces):
    own, right, far_a, far_b, left = pieces
    got_a = move(far_a, 1)
    got_b = move(far_b, -1)
    add = lambda u, v: (u.astype(F32) + v.astype(F32)).astype(BF)
    right = jnp.concatenate([add(right[:HALF], got_a), right[HALF:]], axis=0)
    left = jnp.concatenate([left[:HALF], add(left[HALF:], got_b)], axis=0)
    from_left = move(right, 1)
    from_right = move(left, -1)
    return (own.astype(F32) + from_left.astype(F32) + from_right.astype(F32)).astype(BF)


def exchange(x):
    x = x.reshape(EXP, MAIN, WIDE)
    return lax.all_to_all(x, "expert", split_axis=0, concat_axis=0, tiled=True).reshape(ROWS, WIDE)


def body(tokens, expert_ids, gates, w_gate, w_up, w_down, cotangent):
    d = lax.axis_index("dp").astype(jnp.int32).reshape(1)
    swap = lambda w: lax.ppermute(w, "group", [(0, 1), (1, 0)])
    wg, wu, wd = ((w[0], swap(w[0])) for w in (w_gate, w_up, w_down))
    x, z = pack_call(d, expert_ids, gates, tokens, cotangent)
    xs = gather_dp(exchange(x))
    zs = gather_dp(exchange(z))
    *outs, a, b = fwd_call(d, xs, wg, wu, wd)
    dxs = bwd_call(d, zs, a, b, wg, wu, wd)
    out = exchange(reduce_dp(outs))
    mixed, partial = mix_call(expert_ids, gates, cotangent, out)
    d_gates = (partial + move(partial, 2)) + (move(partial, 1) + move(partial, 3))
    dx = exchange(reduce_dp(dxs))
    d_tokens = dtok_call(expert_ids, dx)
    return mixed, d_tokens, d_gates


def solution(mesh):
    in_specs = (
        P(("group", "expert"), None),
        P(("group", "expert"), None),
        P(("group", "expert"), None),
        P("expert", None, ("dp", "group")),
        P("expert", None, ("dp", "group")),
        P("expert", ("dp", "group"), None),
        P(("group", "expert"), "dp"),
    )
    out_specs = (
        P(("group", "expert"), "dp"),
        P(("group", "expert"), "dp"),
        P(("group", "expert"), None),
    )
    return jax.shard_map(body, mesh=mesh, in_specs=in_specs, out_specs=out_specs, check_vma=False)
```

```python
import functools
import jax
import jax.numpy as jnp
from jax import lax
from jax.experimental import pallas as pl
from jax.experimental.pallas import tpu as pltpu
from jax.sharding import PartitionSpec as P

BF = jnp.bfloat16
F32 = jnp.float32
TOK = 128
EXP = 32
MAIN = 8
OVER = 2
LANE = 128
NDP = 4
D = 3584
QD = D // NDP
CH = QD // LANE
ROWS = EXP * MAIN
WIDE = QD + OVER * LANE
ALL = ROWS + EXP * OVER
HALF = ROWS // 2
HD = 384
VMEM = 24 * 1024 * 1024
COST = pl.CostEstimate(flops=1000, bytes_accessed=1000, transcendentals=0)
LONG_COST = pl.CostEstimate(flops=6_000_000_000, bytes_accessed=1000, transcendentals=0)
NT = (((1,), (1,)), ((), ()))
TN = (((0,), (0,)), ((), ()))


def hbm(x):
    return pltpu.with_memory_space_constraint(x, pltpu.HBM)


def params():
    return pltpu.CompilerParams(vmem_limit_bytes=VMEM)


def iota(shape, dim):
    return lax.broadcasted_iota(jnp.int32, shape, dim)


def dot(a, b, dims=(((1,), (0,)), ((), ()))):
    return lax.dot_general(a, b, dims, preferred_element_type=F32)


def spread(flip):
    shape = (CH * EXP, ROWS) if flip else (ROWS, CH * EXP)
    row, col = iota(shape, int(flip)), iota(shape, 1 - int(flip))
    return ((row % MAIN == col // EXP) & (row // MAIN == col % EXP)).astype(F32).astype(BF)


def pack(over):
    parts = [
        jnp.concatenate([over[c * EXP:(c + 1) * EXP, r * LANE:(r + 1) * LANE] for c in range(OVER)], axis=1)
        for r in range(CH)
    ]
    return dot(spread(False), jnp.concatenate(parts, axis=0)).astype(BF)


def unpack(packed):
    rows = dot(spread(True), packed).astype(BF)
    parts = [
        jnp.concatenate([rows[r * EXP:(r + 1) * EXP, c * LANE:(c + 1) * LANE] for c in range(OVER)], axis=0)
        for r in range(CH)
    ]
    return jnp.concatenate(parts, axis=1)


def join(piece):
    return jnp.concatenate([piece[:, :QD], unpack(piece[:, QD:])], axis=0)


def split(rows):
    return jnp.concatenate([rows[:ROWS], pack(rows[ROWS:])], axis=1)


def columns(rows):
    return [jnp.broadcast_to(rows[k:k + 1], (TOK, TOK)).T for k in range(2)]


def choose(ids):
    lane = iota((TOK, EXP), 1).astype(F32)
    cols = columns(ids.astype(F32))
    hot = [(col[:, :EXP] == lane).astype(F32) for col in cols]
    lower = (iota((TOK, TOK), 1) < iota((TOK, TOK), 0)).astype(F32).astype(BF)
    earlier = dot(lower, (hot[0] + hot[1]).astype(BF))
    out = []
    for k in range(2):
        slot = jnp.sum(earlier * hot[k], axis=1, keepdims=True)
        e = cols[k][:, :1]
        dest = jnp.where(slot < MAIN, e * MAIN + slot, ROWS + (slot - MAIN) * EXP + e).astype(jnp.int32)
        out.append((iota((TOK, ALL), 1) == dest).astype(F32).astype(BF))
    return out


def pack_kernel(d_ref, ids_ref, gates_ref, tok_ref, cot_ref, x_ref, z_ref):
    m0, m1 = choose(ids_ref[...])
    gate = [col[:, :1] for col in columns(gates_ref[...])]
    cot = cot_ref[...].astype(F32)
    x_ref[...] = split(dot(m0 + m1, tok_ref[...], TN).astype(BF))
    z0 = (gate[0] * cot).astype(BF)
    z1 = (gate[1] * cot).astype(BF)
    z_ref[...] = split((dot(m0, z0, TN) + dot(m1, z1, TN)).astype(BF))


def pack_call(d, ids, gates, tokens, cot):
    full = lambda shape: pl.BlockSpec(shape, lambda i, d_ref: (0, 0))
    shape = jax.ShapeDtypeStruct((ROWS, WIDE), BF)
    return pl.pallas_call(
        pack_kernel,
        grid_spec=pltpu.PrefetchScalarGridSpec(
            num_scalar_prefetch=1,
            grid=(1,),
            in_specs=[
                full((2, TOK)),
                full((2, TOK)),
                pl.BlockSpec((TOK, QD), lambda i, d_ref: (0, d_ref[0])),
                full((TOK, QD)),
            ],
            out_specs=[full((ROWS, WIDE))] * 2,
        ),
        out_shape=[shape, shape],
        compiler_params=params(),
        cost_estimate=COST,
    )(d, ids, gates, hbm(tokens), hbm(cot))


def part_of(d, j):
    return pl.ds(pl.multiple_of(((d + j) % NDP) * QD, QD), QD)


NEAR = (0, 1, 3)
FAR = (2,)
IN_W = (QD, 2 * HD)
DOWN_W = (2 * HD, QD)


def fetch(d, pair, buf, sems, pieces, down, i):
    copies = []
    for c, w in enumerate(pair):
        own = pl.ds(c * HD, HD)
        if down:
            src, dst = w.at[:, part_of(d, pieces[i])], buf.at[i, own, :]
        else:
            src, dst = w.at[part_of(d, pieces[i]), :], buf.at[i, :, own]
        copies.append(pltpu.make_async_copy(src, dst, sems.at[i, c]))
        copies[-1].start()
    return copies


def bring(piece, buf, sems, i):
    copy = pltpu.make_async_copy(piece, buf.at[i], sems.at[i])
    copy.start()
    return [copy]


def wait_for(copies):
    for copy in copies:
        copy.wait()


def fwd_near_kernel(
    d_ref, own, high, low, wg0, wg1, wu0, wu1, a_ref, b_ref, gate, up, slots, gate_sem, up_sem, slot_sem
):
    d = d_ref[0]
    copies = []
    for i, piece in enumerate((own, high, low)):
        copies.append((
            bring(piece, slots, slot_sem, i),
            fetch(d, (wg0, wg1), gate, gate_sem, NEAR, False, i),
            fetch(d, (wu0, wu1), up, up_sem, NEAR, False, i),
        ))
    for i, (slot, *both) in enumerate(copies):
        wait_for(slot)
        rows = join(slots[i])
        for out, weights, buf in ((a_ref, both[0], gate), (b_ref, both[1], up)):
            wait_for(weights)
            part = dot(rows, buf[i])
            out[...] = part if i == 0 else out[...] + part


def fwd_far_kernel(
    d_ref, far_a, far_b, a_in, b_in, wg0, wg1, wu0, wu1, wd0, wd1,
    a_ref, b_ref, h_ref, out_a, out_b, gate, up, down, gate_sem, up_sem, down_sem,
):
    d = d_ref[0]
    gates = fetch(d, (wg0, wg1), gate, gate_sem, FAR, False, 0)
    ups = fetch(d, (wu0, wu1), up, up_sem, FAR, False, 0)
    downs = fetch(d, (wd0, wd1), down, down_sem, FAR, True, 0)
    rows = join(jnp.concatenate([far_a[...], far_b[...]], axis=0))
    wait_for(gates)
    a_ref[...] = a_in[...] + dot(rows, gate[0])
    wait_for(ups)
    b_ref[...] = b_in[...] + dot(rows, up[0])
    a, b = a_ref[...], b_ref[...]
    h_ref[...] = (a * jax.nn.sigmoid(a) * b).astype(BF)
    wait_for(downs)
    out = split(dot(h_ref[...], down[0]).astype(BF))
    out_a[...] = out[:HALF]
    out_b[...] = out[HALF:]


def fwd_rest_kernel(d_ref, h_ref, wd0, wd1, own, high, low, down, down_sem):
    downs = [fetch(d_ref[0], (wd0, wd1), down, down_sem, NEAR, True, i) for i in range(len(NEAR))]
    for i, ref in enumerate((own, high, low)):
        wait_for(downs[i])
        ref[...] = split(dot(h_ref[...], down[i]).astype(BF))


def bwd_near_kernel(d_ref, own, high, low, wd0, wd1, g_ref, down, slots, down_sem, slot_sem):
    copies = []
    for i, piece in enumerate((own, high, low)):
        copies.append((
            bring(piece, slots, slot_sem, i),
            fetch(d_ref[0], (wd0, wd1), down, down_sem, NEAR, True, i),
        ))
    for i, (slot, weights) in enumerate(copies):
        wait_for(slot)
        rows = join(slots[i])
        wait_for(weights)
        part = dot(rows, down[i], NT)
        g_ref[...] = part if i == 0 else g_ref[...] + part


def bwd_far_kernel(
    d_ref, far_a, far_b, g_in, a_ref, b_ref, wg0, wg1, wu0, wu1, wd0, wd1,
    da_ref, db_ref, out_a, out_b, gate, up, down, gate_sem, up_sem, down_sem,
):
    d = d_ref[0]
    downs = fetch(d, (wd0, wd1), down, down_sem, FAR, True, 0)
    gates = fetch(d, (wg0, wg1), gate, gate_sem, FAR, False, 0)
    ups = fetch(d, (wu0, wu1), up, up_sem, FAR, False, 0)
    rows = join(jnp.concatenate([far_a[...], far_b[...]], axis=0))
    wait_for(downs)
    g = g_in[...] + dot(rows, down[0], NT)
    a, b = a_ref[...], b_ref[...]
    s = jax.nn.sigmoid(a)
    da_ref[...] = (g * b * s * (1.0 + a * (1.0 - s))).astype(BF)
    db_ref[...] = (g * a * s).astype(BF)
    wait_for(gates)
    wait_for(ups)
    out = split((dot(da_ref[...], gate[0], NT) + dot(db_ref[...], up[0], NT)).astype(BF))
    out_a[...] = out[:HALF]
    out_b[...] = out[HALF:]


def bwd_rest_kernel(d_ref, da_ref, db_ref, wg0, wg1, wu0, wu1, own, high, low, gate, up, gate_sem, up_sem):
    d = d_ref[0]
    copies = [
        fetch(d, (wg0, wg1), gate, gate_sem, NEAR, False, i) + fetch(d, (wu0, wu1), up, up_sem, NEAR, False, i)
        for i in range(len(NEAR))
    ]
    for i, ref in enumerate((own, high, low)):
        wait_for(copies[i])
        ref[...] = split((dot(da_ref[...], gate[i], NT) + dot(db_ref[...], up[i], NT)).astype(BF))


INSIDE = pl.BlockSpec(memory_space=pltpu.VMEM)
OUTSIDE = pl.BlockSpec(memory_space=pltpu.HBM)
HIDDEN = (ALL, 2 * HD)


def expert_call(kernel, d, ins, weights, outs, buffers, pieces, slots=()):
    count = len(pieces)
    space = [pltpu.VMEM((count, *shape), BF) for shape in buffers]
    sems = [pltpu.SemaphoreType.DMA((count, 2)) for _ in buffers]
    if slots:
        space.append(pltpu.VMEM((len(slots), ROWS, WIDE), BF))
        sems.append(pltpu.SemaphoreType.DMA((len(slots),)))
    return pl.pallas_call(
        kernel,
        in_specs=[pl.BlockSpec(memory_space=pltpu.SMEM)]
        + [OUTSIDE] * len(slots) + [INSIDE] * len(ins) + [OUTSIDE] * len(weights),
        out_specs=[INSIDE] * len(outs),
        out_shape=[jax.ShapeDtypeStruct(shape, kind) for shape, kind in outs],
        scratch_shapes=space + sems,
        compiler_params=params(),
        cost_estimate=COST if kernel in (fwd_far_kernel, fwd_rest_kernel, bwd_far_kernel) else LONG_COST,
    )(d, *slots, *ins, *weights)


def halves_kernel(high, low, low_a, high_b, sems):
    copies = [
        pltpu.make_async_copy(low.at[pl.ds(0, HALF), :], low_a, sems.at[0]),
        pltpu.make_async_copy(high.at[pl.ds(HALF, HALF), :], high_b, sems.at[1]),
    ]
    for copy in copies:
        copy.start()
    for copy in copies:
        copy.wait()


def halves_call(high, low):
    return pl.pallas_call(
        halves_kernel,
        in_specs=[OUTSIDE] * 2,
        out_specs=[INSIDE] * 2,
        out_shape=[jax.ShapeDtypeStruct((HALF, WIDE), BF)] * 2,
        scratch_shapes=[pltpu.SemaphoreType.DMA((2,))],
        compiler_params=params(),
        cost_estimate=COST,
    )(high, low)


SLOT_ROWS = ((ROWS, WIDE), BF)
HALF_ROWS = ((HALF, WIDE), BF)
SUMS = (HIDDEN, F32)
UNITS = (HIDDEN, BF)


def mix_kernel(ids_ref, gates_ref, cot_ref, out_ref, mixed_ref, dg_ref):
    hots = choose(ids_ref[...])
    rows = join(out_ref[...])
    gate = [col[:, :1] for col in columns(gates_ref[...])]
    cot = cot_ref[...].astype(F32)
    mixed = jnp.zeros((TOK, QD), F32)
    for k in range(2):
        mine = dot(hots[k], rows)
        mixed = mixed + gate[k] * mine
        dg_ref[:, k:k + 1] = jnp.sum(cot * mine, axis=1, keepdims=True)
    mixed_ref[...] = mixed.astype(BF)


def mix_call(ids, gates, cot, out):
    return pl.pallas_call(
        mix_kernel,
        out_shape=[jax.ShapeDtypeStruct((TOK, QD), BF), jax.ShapeDtypeStruct((TOK, 2), F32)],
        compiler_params=params(),
        cost_estimate=COST,
    )(ids, gates, cot, out)


def dtok_kernel(ids_ref, dx_ref, out_ref):
    m0, m1 = choose(ids_ref[...])
    out_ref[...] = dot(m0 + m1, join(dx_ref[...])).astype(BF)


def dtok_call(ids, dx):
    return pl.pallas_call(
        dtok_kernel,
        out_shape=jax.ShapeDtypeStruct((TOK, QD), BF),
        compiler_params=params(),
        cost_estimate=COST,
    )(ids, dx)


def move(x, by):
    return lax.ppermute(x, "dp", [(i, (i + by) % NDP) for i in range(NDP)])


def gather_near(own):
    return move(own, -1), move(own, 1)


def gather_far(high, low):
    low_a, high_b = halves_call(high, low)
    return move(low_a, 1), move(high_b, -1)


def local_call(kernel, outs, *ins):
    return pl.pallas_call(
        kernel,
        out_shape=[jax.ShapeDtypeStruct(shape, kind) for shape, kind in outs],
        compiler_params=params(),
        cost_estimate=COST,
    )(*ins)


def add(*terms):
    total = terms[0].astype(F32)
    for term in terms[1:]:
        total = total + term.astype(F32)
    return total.astype(BF)


def add_far_kernel(high, low, got_a, got_b, high_out, low_out):
    high_out[:HALF] = add(high[:HALF], got_a[...])
    high_out[HALF:] = high[HALF:]
    low_out[:HALF] = low[:HALF]
    low_out[HALF:] = add(low[HALF:], got_b[...])


def add_near_kernel(own, from_low, from_high, out):
    out[...] = add(own[...], from_low[...], from_high[...])


def reduce_far(far_a, far_b):
    return move(far_a, 1), move(far_b, -1)


def reduce_near(high, low, got_a, got_b):
    high, low = local_call(add_far_kernel, [SLOT_ROWS] * 2, high, low, got_a, got_b)
    return move(high, 1), move(low, -1)


def finish(own, from_low, from_high):
    return local_call(add_near_kernel, [SLOT_ROWS], own, from_low, from_high)[0]


def exchange(x):
    x = x.reshape(EXP, MAIN, WIDE)
    return lax.all_to_all(x, "expert", split_axis=0, concat_axis=0, tiled=True).reshape(ROWS, WIDE)


def after(x, *others):
    return lax.optimization_barrier((x, *others))[0]


def body(tokens, expert_ids, gates, w_gate, w_up, w_down, cotangent):
    d = lax.axis_index("dp").astype(jnp.int32).reshape(1)
    swap = lambda w: lax.ppermute(w, "group", [(0, 1), (1, 0)])
    wg, wu, wd = ((hbm(w[0]), hbm(swap(w[0]))) for w in (w_gate, w_up, w_down))
    ids, gates = expert_ids.T, gates.T
    x_pack, z_pack = pack_call(d, ids, gates, tokens, cotangent)
    x_own = exchange(x_pack)
    z_own = exchange(after(z_pack, x_own))
    x_own = hbm(x_own)
    x_high, x_low = map(hbm, gather_near(x_own))
    x_far = gather_far(x_high, x_low)
    z_own = hbm(z_own)
    a, b = expert_call(
        fwd_near_kernel, d, (), (*wg, *wu), [SUMS] * 2, [IN_W] * 2, NEAR, (after(x_own, z_own), x_high, x_low)
    )
    z_high, z_low = map(hbm, gather_near(z_own))
    a, b, h, far_a, far_b = expert_call(
        fwd_far_kernel, d, (*x_far, a, b), (*wg, *wu, *wd),
        [SUMS, SUMS, UNITS, HALF_ROWS, HALF_ROWS], [IN_W, IN_W, DOWN_W], FAR,
    )
    got = reduce_far(far_a, far_b)
    out_own, out_high, out_low = expert_call(
        fwd_rest_kernel, d, (h,), wd, [SLOT_ROWS] * 3, [DOWN_W], NEAR
    )
    z_far = gather_far(z_high, z_low)
    out_low = after(out_low, z_high, z_low)
    from_low, from_high = reduce_near(out_high, out_low, *got)
    (g,) = expert_call(bwd_near_kernel, d, (), wd, [SUMS], [DOWN_W], NEAR, (z_own, z_high, z_low))
    da, db, far_a, far_b = expert_call(
        bwd_far_kernel, d, (*z_far, g, a, b), (*wg, *wu, *wd),
        [UNITS, UNITS, HALF_ROWS, HALF_ROWS], [IN_W, IN_W, DOWN_W], FAR,
    )
    got = reduce_far(far_a, far_b)
    dx_own, dx_high, dx_low = expert_call(
        bwd_rest_kernel, d, (da, db), (*wg, *wu), [SLOT_ROWS] * 3, [IN_W] * 2, NEAR
    )
    from_low = after(from_low, dx_own, *got)
    out = exchange(finish(out_own, from_low, from_high))
    from_low, from_high = reduce_near(dx_high, dx_low, *got)
    dx = exchange(finish(dx_own, from_low, from_high))
    mixed, partial = mix_call(ids, gates, cotangent, out)
    d_gates = (partial + move(partial, 2)) + (move(partial, 1) + move(partial, 3))
    d_tokens = dtok_call(ids, dx)
    return mixed, d_tokens, d_gates


def solution(mesh):
    in_specs = (
        P(("group", "expert"), None),
        P(("group", "expert"), None),
        P(("group", "expert"), None),
        P("expert", None, ("dp", "group")),
        P("expert", None, ("dp", "group")),
        P("expert", ("dp", "group"), None),
        P(("group", "expert"), "dp"),
    )
    out_specs = (
        P(("group", "expert"), "dp"),
        P(("group", "expert"), "dp"),
        P(("group", "expert"), None),
    )
    return jax.shard_map(body, mesh=mesh, in_specs=in_specs, out_specs=out_specs, check_vma=False)
```

```python
import functools
import jax
import jax.numpy as jnp
from jax import lax
from jax.experimental import pallas as pl
from jax.experimental.pallas import tpu as pltpu
from jax.sharding import PartitionSpec as P

BF = jnp.bfloat16
F32 = jnp.float32
TOK = 128
EXP = 32
MAIN = 8
OVER = 2
LANE = 128
NDP = 4
D = 3584
QD = D // NDP
CH = QD // LANE
ROWS = EXP * MAIN
WIDE = QD + OVER * LANE
ALL = ROWS + EXP * OVER
HALF = ROWS // 2
HD = 384
VMEM = 20 * 1024 * 1024
MOST = 56 * 1024 * 1024
COST = pl.CostEstimate(flops=1000, bytes_accessed=1000, transcendentals=0)
LONG_COST = pl.CostEstimate(flops=6_000_000_000, bytes_accessed=1000, transcendentals=0)
NT = (((1,), (1,)), ((), ()))
TN = (((0,), (0,)), ((), ()))


def hbm(x):
    return pltpu.with_memory_space_constraint(x, pltpu.HBM)


def params(limit=VMEM):
    return pltpu.CompilerParams(vmem_limit_bytes=limit)


def iota(shape, dim):
    return lax.broadcasted_iota(jnp.int32, shape, dim)


def dot(a, b, dims=(((1,), (0,)), ((), ()))):
    return lax.dot_general(a, b, dims, preferred_element_type=F32)


def spread(flip):
    shape = (CH * EXP, ROWS) if flip else (ROWS, CH * EXP)
    row, col = iota(shape, int(flip)), iota(shape, 1 - int(flip))
    return ((row % MAIN == col // EXP) & (row // MAIN == col % EXP)).astype(F32).astype(BF)


def pack(over):
    parts = [
        jnp.concatenate([over[c * EXP:(c + 1) * EXP, r * LANE:(r + 1) * LANE] for c in range(OVER)], axis=1)
        for r in range(CH)
    ]
    return dot(spread(False), jnp.concatenate(parts, axis=0)).astype(BF)


def unpack(packed):
    rows = dot(spread(True), packed).astype(BF)
    parts = [
        jnp.concatenate([rows[r * EXP:(r + 1) * EXP, c * LANE:(c + 1) * LANE] for c in range(OVER)], axis=0)
        for r in range(CH)
    ]
    return jnp.concatenate(parts, axis=1)


def join(piece):
    return jnp.concatenate([piece[:, :QD], unpack(piece[:, QD:])], axis=0)


def split(rows):
    return jnp.concatenate([rows[:ROWS], pack(rows[ROWS:])], axis=1)


def columns(rows):
    return [jnp.broadcast_to(rows[k:k + 1], (TOK, TOK)).T for k in range(2)]


def choose(ids):
    lane = iota((TOK, EXP), 1).astype(F32)
    cols = columns(ids.astype(F32))
    hot = [(col[:, :EXP] == lane).astype(F32) for col in cols]
    lower = (iota((TOK, TOK), 1) < iota((TOK, TOK), 0)).astype(F32).astype(BF)
    earlier = dot(lower, (hot[0] + hot[1]).astype(BF))
    out = []
    for k in range(2):
        slot = jnp.sum(earlier * hot[k], axis=1, keepdims=True)
        e = cols[k][:, :1]
        dest = jnp.where(slot < MAIN, e * MAIN + slot, ROWS + (slot - MAIN) * EXP + e).astype(jnp.int32)
        out.append((iota((TOK, ALL), 1) == dest).astype(F32).astype(BF))
    return out


def choose_rows(ids):
    lane = iota((EXP, TOK), 0)
    hot = [(lane == ids[k:k + 1]).astype(F32) for k in range(2)]
    upper = (iota((TOK, TOK), 0) < iota((TOK, TOK), 1)).astype(F32).astype(BF)
    earlier = dot((hot[0] + hot[1]).astype(BF), upper)
    out = []
    for k in range(2):
        slot = jnp.sum(earlier * hot[k], axis=0, keepdims=True).astype(jnp.int32)
        e = ids[k:k + 1]
        dest = jnp.where(slot < MAIN, e * MAIN + slot, ROWS + (slot - MAIN) * EXP + e)
        out.append((iota((ALL, TOK), 0) == dest).astype(F32))
    return out


def pack_kernel(d_ref, ids_ref, gates_ref, tok_ref, cot_ref, x_ref, z_ref):
    m0, m1 = choose_rows(ids_ref[...])
    gates = gates_ref[...]
    hot = (m0 + m1).astype(BF)
    x_ref[...] = split(dot(hot, tok_ref[...]).astype(BF))
    gate = jnp.sum(m0 * gates[0:1] + m1 * gates[1:2], axis=1, keepdims=True)
    z_ref[...] = split((gate * dot(hot, cot_ref[...])).astype(BF))


def pack_call(d, ids, gates, tokens, cot):
    full = lambda shape: pl.BlockSpec(shape, lambda i, d_ref: (0, 0))
    shape = jax.ShapeDtypeStruct((ROWS, WIDE), BF)
    return pl.pallas_call(
        pack_kernel,
        grid_spec=pltpu.PrefetchScalarGridSpec(
            num_scalar_prefetch=1,
            grid=(1,),
            in_specs=[
                full((2, TOK)),
                full((2, TOK)),
                pl.BlockSpec((TOK, QD), lambda i, d_ref: (0, d_ref[0])),
                full((TOK, QD)),
            ],
            out_specs=[full((ROWS, WIDE))] * 2,
        ),
        out_shape=[shape, shape],
        compiler_params=params(MOST),
        cost_estimate=COST,
    )(d, hbm(ids), hbm(gates), hbm(tokens), hbm(cot))


def touch_kernel(x_ref, out_ref):
    out_ref[...] = jnp.zeros_like(out_ref)


def touch_call(x):
    return pl.pallas_call(
        touch_kernel,
        in_specs=[pl.BlockSpec(memory_space=pl.ANY)],
        out_shape=jax.ShapeDtypeStruct((8, LANE), F32),
        compiler_params=params(),
        cost_estimate=LONG_COST,
    )(x)


def part_of(d, j):
    return pl.ds(pl.multiple_of(((d + j) % NDP) * QD, QD), QD)


NEAR = (0, 1, 3)
FAR = (2,)
IN_W = (QD, 2 * HD)
DOWN_W = (2 * HD, QD)


def fetch(d, pair, buf, sems, pieces, down, i):
    copies = []
    for c, w in enumerate(pair):
        own = pl.ds(c * HD, HD)
        if down:
            src, dst = w.at[:, part_of(d, pieces[i])], buf.at[i, own, :]
        else:
            src, dst = w.at[part_of(d, pieces[i]), :], buf.at[i, :, own]
        copies.append(pltpu.make_async_copy(src, dst, sems.at[i, c]))
        copies[-1].start()
    return copies


def bring(src, dst, sem):
    copy = pltpu.make_async_copy(src, dst, sem)
    copy.start()
    return copy


def wait_for(copies):
    for copy in copies:
        copy.wait()


def fetch_all(d, pair, buf, sems, pieces, down):
    return [fetch(d, pair, buf, sems, pieces, down, i) for i in range(len(pieces))]


def fwd_near_kernel(d_ref, own, high, low, wg0, wg1, wu0, wu1, sums, gate, up, gate_sem, up_sem):
    d = d_ref[0]
    weights = []
    for i in range(len(NEAR)):
        weights.append(fetch(d, (wg0, wg1), gate, gate_sem, NEAR, False, i))
        weights.append(fetch(d, (wu0, wu1), up, up_sem, NEAR, False, i))
    for i, piece in enumerate((own, high, low)):
        rows = join(piece[...])
        for k, buf in enumerate((gate, up)):
            wait_for(weights[2 * i + k])
            part = dot(rows, buf[i])
            sums[k] = part if i == 0 else sums[k] + part


def fwd_far_kernel(
    d_ref, far_a, far_b, wg0, wg1, wu0, wu1, wd0, wd1, sums,
    a_ref, b_ref, h_ref, out_a, out_b, gate, up, down, near, gate_sem, up_sem, down_sem, near_sem, in_sem,
):
    d = d_ref[0]
    gates = fetch(d, (wg0, wg1), gate, gate_sem, FAR, False, 0)
    ups = fetch(d, (wu0, wu1), up, up_sem, FAR, False, 0)
    a_copy = bring(sums.at[0], a_ref, in_sem.at[0])
    b_copy = bring(sums.at[1], b_ref, in_sem.at[1])
    downs = fetch(d, (wd0, wd1), down, down_sem, FAR, True, 0)
    nears = fetch_all(d, (wd0, wd1), near, near_sem, NEAR, True)
    rows = join(jnp.concatenate([far_a[...], far_b[...]], axis=0))
    wait_for(gates)
    part = dot(rows, gate[0])
    a_copy.wait()
    a_ref[...] = a_ref[...] + part
    wait_for(ups)
    part = dot(rows, up[0])
    b_copy.wait()
    b_ref[...] = b_ref[...] + part
    a, b = a_ref[...], b_ref[...]
    h_ref[...] = (a * jax.nn.sigmoid(a) * b).astype(BF)
    wait_for(downs)
    out = split(dot(h_ref[...], down[0]).astype(BF))
    out_a[...] = out[:HALF]
    out_b[...] = out[HALF:]
    for copies in nears:
        wait_for(copies)


def fwd_rest_kernel(d_ref, h_ref, down, wg0, wg1, own, high, low, gate, gate_sem):
    copies = fetch_all(d_ref[0], (wg0, wg1), gate, gate_sem, NEAR, False)
    for i, ref in enumerate((own, high, low)):
        ref[...] = split(dot(h_ref[...], down[i]).astype(BF))
    for copy in copies:
        wait_for(copy)


def bwd_near_kernel(d_ref, own, high, low, down, wu0, wu1, g_ref, up, up_sem):
    copies = fetch_all(d_ref[0], (wu0, wu1), up, up_sem, NEAR, False)
    for i, piece in enumerate((own, high, low)):
        part = dot(join(piece[...]), down[i], NT)
        g_ref[...] = part if i == 0 else g_ref[...] + part
    for copy in copies:
        wait_for(copy)


def bwd_far_kernel(d_ref, far_a, far_b, g_in, a_ref, b_ref, gate, up, down, da_ref, db_ref, out_a, out_b):
    rows = join(jnp.concatenate([far_a[...], far_b[...]], axis=0))
    g = g_in[...] + dot(rows, down[0], NT)
    a, b = a_ref[...], b_ref[...]
    s = jax.nn.sigmoid(a)
    da_ref[...] = (g * b * s * (1.0 + a * (1.0 - s))).astype(BF)
    db_ref[...] = (g * a * s).astype(BF)
    out = split((dot(da_ref[...], gate[0], NT) + dot(db_ref[...], up[0], NT)).astype(BF))
    out_a[...] = out[:HALF]
    out_b[...] = out[HALF:]


def bwd_rest_kernel(d_ref, da_ref, db_ref, gate, up, own, high, low):
    for i, ref in enumerate((own, high, low)):
        ref[...] = split((dot(da_ref[...], gate[i], NT) + dot(db_ref[...], up[i], NT)).astype(BF))


INSIDE = pl.BlockSpec(memory_space=pltpu.VMEM)
OUTSIDE = pl.BlockSpec(memory_space=pltpu.HBM)
HIDDEN = (ALL, 2 * HD)


def sems(*shape):
    return pltpu.SemaphoreType.DMA(shape)


def expert_call(kernel, d, inside, outside, outs, scratch=(), far_outs=()):
    return pl.pallas_call(
        kernel,
        in_specs=[pl.BlockSpec(memory_space=pltpu.SMEM)] + [INSIDE] * len(inside) + [OUTSIDE] * len(outside),
        out_specs=[INSIDE] * len(outs) + [OUTSIDE] * len(far_outs),
        out_shape=[jax.ShapeDtypeStruct(shape, kind) for shape, kind in (*outs, *far_outs)],
        scratch_shapes=list(scratch),
        compiler_params=params(),
        cost_estimate=COST if kernel in (fwd_far_kernel, fwd_rest_kernel, bwd_far_kernel) else LONG_COST,
    )(d, *inside, *outside)


def halves_kernel(high, low, low_a, high_b):
    low_a[...] = low[:HALF]
    high_b[...] = high[HALF:]


def halves_call(high, low):
    return local_call(halves_kernel, [HALF_ROWS] * 2, high, low)


SLOT_ROWS = ((ROWS, WIDE), BF)
HALF_ROWS = ((HALF, WIDE), BF)
SUMS = (HIDDEN, F32)
UNITS = (HIDDEN, BF)


def mix_kernel(ids_ref, gates_ref, cot_ref, out_ref, mixed_ref, dg_ref, hot_ref):
    hots = choose(ids_ref[...])
    hot_ref[...] = hots[0] + hots[1]
    rows = join(out_ref[...])
    gate = [col[:, :1] for col in columns(gates_ref[...])]
    cot = cot_ref[...].astype(F32)
    mixed = jnp.zeros((TOK, QD), F32)
    for k in range(2):
        mine = dot(hots[k], rows)
        mixed = mixed + gate[k] * mine
        dg_ref[:, k:k + 1] = jnp.sum(cot * mine, axis=1, keepdims=True)
    mixed_ref[...] = mixed.astype(BF)


def mix_call(ids, gates, cot, out):
    return pl.pallas_call(
        mix_kernel,
        out_shape=[
            jax.ShapeDtypeStruct((TOK, QD), BF),
            jax.ShapeDtypeStruct((TOK, 2), F32),
            jax.ShapeDtypeStruct((TOK, ALL), BF),
        ],
        compiler_params=params(),
        cost_estimate=COST,
    )(ids, gates, cot, out)


def dtok_kernel(hot_ref, dx_ref, out_ref):
    out_ref[...] = dot(hot_ref[...], join(dx_ref[...])).astype(BF)


def dtok_call(hot, dx):
    return pl.pallas_call(
        dtok_kernel,
        out_shape=jax.ShapeDtypeStruct((TOK, QD), BF),
        compiler_params=params(),
        cost_estimate=COST,
    )(hot, dx)


def move(x, by):
    return lax.ppermute(x, "dp", [(i, (i + by) % NDP) for i in range(NDP)])


def gather_near(own):
    return move(own, -1), move(own, 1)


def gather_far(high, low):
    low_a, high_b = halves_call(high, low)
    return move(low_a, 1), move(high_b, -1)


def local_call(kernel, outs, *ins):
    return pl.pallas_call(
        kernel,
        out_shape=[jax.ShapeDtypeStruct(shape, kind) for shape, kind in outs],
        compiler_params=params(),
        cost_estimate=COST,
    )(*ins)


def add(*terms):
    total = terms[0].astype(F32)
    for term in terms[1:]:
        total = total + term.astype(F32)
    return total.astype(BF)


def add_far_kernel(high, low, got_a, got_b, high_out, low_out):
    high_out[:HALF] = add(high[:HALF], got_a[...])
    high_out[HALF:] = high[HALF:]
    low_out[:HALF] = low[:HALF]
    low_out[HALF:] = add(low[HALF:], got_b[...])


def add_near_kernel(own, from_low, from_high, out):
    out[...] = add(own[...], from_low[...], from_high[...])


def reduce_far(far_a, far_b):
    return move(far_a, 1), move(far_b, -1)


def reduce_near(high, low, got_a, got_b):
    high, low = local_call(add_far_kernel, [SLOT_ROWS] * 2, high, low, got_a, got_b)
    return move(high, 1), move(low, -1)


def finish(own, from_low, from_high):
    return local_call(add_near_kernel, [SLOT_ROWS], own, from_low, from_high)[0]


def exchange(x):
    x = x.reshape(EXP, MAIN, WIDE)
    return lax.all_to_all(x, "expert", split_axis=0, concat_axis=0, tiled=True).reshape(ROWS, WIDE)


def after(x, *others):
    return lax.optimization_barrier((x, *others))[0]


def body(tokens, expert_ids, gates, w_gate, w_up, w_down, cotangent):
    d = lax.axis_index("dp").astype(jnp.int32).reshape(1)
    swap = lambda w: lax.ppermute(w, "group", [(0, 1), (1, 0)])
    wg, wu, wd = ((hbm(w[0]), hbm(swap(w[0]))) for w in (w_gate, w_up, w_down))
    ids, gates = expert_ids.T, gates.T
    x_pack, z_pack = pack_call(d, ids, gates, tokens, cotangent)
    x_own = exchange(x_pack)
    x_high, x_low = gather_near(x_own)
    z_own = exchange(after(z_pack, touch_call(x_own)))
    x_far = gather_far(x_high, x_low)
    (sums,) = expert_call(
        fwd_near_kernel, d, (x_own, x_high, x_low), (*wg, *wu), [((2, *HIDDEN), F32)],
        [pltpu.VMEM((3, *IN_W), BF)] * 2 + [sems(3, 2), sems(3, 2)],
    )
    z_own = after(z_own, sums, *x_far)
    z_high, z_low = gather_near(z_own)
    a, b, h, far_a, far_b, gate_far, up_far, down_far, down_near = expert_call(
        fwd_far_kernel, d, x_far, (*wg, *wu, *wd, hbm(sums)),
        [SUMS, SUMS, UNITS, HALF_ROWS, HALF_ROWS, *(((1, *w), BF) for w in (IN_W, IN_W, DOWN_W)), ((3, *DOWN_W), BF)],
        [sems(1, 2), sems(1, 2), sems(1, 2), sems(3, 2), sems(2)],
    )
    got = reduce_far(far_a, far_b)
    out_own, out_high, out_low, gate_near = expert_call(
        fwd_rest_kernel, d, (h, down_near), wg, [SLOT_ROWS] * 3 + [((3, *IN_W), BF)], [sems(3, 2)]
    )
    z_far = gather_far(z_high, z_low)
    g, up_near = expert_call(
        bwd_near_kernel, d, (z_own, z_high, z_low, down_near), wu, [SUMS, ((3, *IN_W), BF)], [sems(3, 2)]
    )
    out_low = after(out_low, g)
    from_low, from_high = reduce_near(out_high, out_low, *got)
    da, db, far_a, far_b = expert_call(
        bwd_far_kernel, d, (*z_far, g, a, b, gate_far, up_far, down_far), (),
        [UNITS, UNITS, HALF_ROWS, HALF_ROWS],
    )
    got = reduce_far(far_a, far_b)
    dx_own, dx_high, dx_low = expert_call(
        bwd_rest_kernel, d, (da, db, gate_near, up_near), (), [SLOT_ROWS] * 3
    )
    out = exchange(after(finish(out_own, from_low, from_high), dx_own, *got))
    from_low, from_high = reduce_near(dx_high, dx_low, *got)
    dx = exchange(finish(dx_own, from_low, from_high))
    mixed, partial, hot = mix_call(ids, gates, cotangent, out)
    d_gates = (partial + move(partial, 2)) + (move(partial, 1) + move(partial, 3))
    d_tokens = dtok_call(hot, dx)
    return mixed, d_tokens, d_gates


def solution(mesh):
    in_specs = (
        P(("group", "expert"), None),
        P(("group", "expert"), None),
        P(("group", "expert"), None),
        P("expert", None, ("dp", "group")),
        P("expert", None, ("dp", "group")),
        P("expert", ("dp", "group"), None),
        P(("group", "expert"), "dp"),
    )
    out_specs = (
        P(("group", "expert"), "dp"),
        P(("group", "expert"), "dp"),
        P(("group", "expert"), None),
    )
    return jax.shard_map(body, mesh=mesh, in_specs=in_specs, out_specs=out_specs, check_vma=False)
```

```python
import functools
import jax
import jax.numpy as jnp
from jax import lax
from jax.experimental import pallas as pl
from jax.experimental.pallas import tpu as pltpu
from jax.sharding import PartitionSpec as P

BF = jnp.bfloat16
F32 = jnp.float32
TOK = 128
EXP = 32
MAIN = 8
OVER = 2
LANE = 128
NDP = 4
D = 3584
QD = D // NDP
CH = QD // LANE
ROWS = EXP * MAIN
WIDE = QD + OVER * LANE
ALL = ROWS + EXP * OVER
HALF = ROWS // 2
HD = 384
VMEM = 20 * 1024 * 1024
MOST = 56 * 1024 * 1024
COST = pl.CostEstimate(flops=1000, bytes_accessed=1000, transcendentals=0)
LONG_COST = pl.CostEstimate(flops=6_000_000_000, bytes_accessed=1000, transcendentals=0)
NT = (((1,), (1,)), ((), ()))
TN = (((0,), (0,)), ((), ()))


def hbm(x):
    return pltpu.with_memory_space_constraint(x, pltpu.HBM)


def params(limit=VMEM):
    return pltpu.CompilerParams(vmem_limit_bytes=limit)


def iota(shape, dim):
    return lax.broadcasted_iota(jnp.int32, shape, dim)


def dot(a, b, dims=(((1,), (0,)), ((), ()))):
    return lax.dot_general(a, b, dims, preferred_element_type=F32)


def spread(flip):
    shape = (CH * EXP, ROWS) if flip else (ROWS, CH * EXP)
    row, col = iota(shape, int(flip)), iota(shape, 1 - int(flip))
    return ((row % MAIN == col // EXP) & (row // MAIN == col % EXP)).astype(F32).astype(BF)


def pack(over):
    parts = [
        jnp.concatenate([over[c * EXP:(c + 1) * EXP, r * LANE:(r + 1) * LANE] for c in range(OVER)], axis=1)
        for r in range(CH)
    ]
    return dot(spread(False), jnp.concatenate(parts, axis=0)).astype(BF)


def unpack(packed):
    rows = dot(spread(True), packed).astype(BF)
    parts = [
        jnp.concatenate([rows[r * EXP:(r + 1) * EXP, c * LANE:(c + 1) * LANE] for c in range(OVER)], axis=0)
        for r in range(CH)
    ]
    return jnp.concatenate(parts, axis=1)


def join(piece):
    return jnp.concatenate([piece[:, :QD], unpack(piece[:, QD:])], axis=0)


def split(rows):
    return jnp.concatenate([rows[:ROWS], pack(rows[ROWS:])], axis=1)


def columns(rows):
    return [jnp.broadcast_to(rows[k:k + 1], (TOK, TOK)).T for k in range(2)]


def choose(ids):
    lane = iota((TOK, EXP), 1).astype(F32)
    cols = columns(ids.astype(F32))
    hot = [(col[:, :EXP] == lane).astype(F32) for col in cols]
    lower = (iota((TOK, TOK), 1) < iota((TOK, TOK), 0)).astype(F32).astype(BF)
    earlier = dot(lower, (hot[0] + hot[1]).astype(BF))
    out = []
    for k in range(2):
        slot = jnp.sum(earlier * hot[k], axis=1, keepdims=True)
        e = cols[k][:, :1]
        dest = jnp.where(slot < MAIN, e * MAIN + slot, ROWS + (slot - MAIN) * EXP + e).astype(jnp.int32)
        out.append((iota((TOK, ALL), 1) == dest).astype(F32).astype(BF))
    return out


def choose_rows(ids):
    lane = iota((EXP, TOK), 0)
    hot = [(lane == ids[k:k + 1]).astype(F32) for k in range(2)]
    upper = (iota((TOK, TOK), 0) < iota((TOK, TOK), 1)).astype(F32).astype(BF)
    earlier = dot((hot[0] + hot[1]).astype(BF), upper)
    out = []
    for k in range(2):
        slot = jnp.sum(earlier * hot[k], axis=0, keepdims=True).astype(jnp.int32)
        e = ids[k:k + 1]
        dest = jnp.where(slot < MAIN, e * MAIN + slot, ROWS + (slot - MAIN) * EXP + e)
        out.append((iota((ALL, TOK), 0) == dest).astype(F32))
    return out


def pack_kernel(d_ref, ids_ref, gates_ref, tok_ref, cot_ref, x_ref, z_ref):
    m0, m1 = choose_rows(ids_ref[...])
    gates = gates_ref[...]
    hot = (m0 + m1).astype(BF)
    x_ref[...] = split(dot(hot, tok_ref[...]).astype(BF))
    gate = jnp.sum(m0 * gates[0:1] + m1 * gates[1:2], axis=1, keepdims=True)
    z_ref[...] = split((gate * dot(hot, cot_ref[...])).astype(BF))


def pack_call(d, ids, gates, tokens, cot):
    full = lambda shape: pl.BlockSpec(shape, lambda i, d_ref: (0, 0))
    shape = jax.ShapeDtypeStruct((ROWS, WIDE), BF)
    return pl.pallas_call(
        pack_kernel,
        grid_spec=pltpu.PrefetchScalarGridSpec(
            num_scalar_prefetch=1,
            grid=(1,),
            in_specs=[
                full((2, TOK)),
                full((2, TOK)),
                pl.BlockSpec((TOK, QD), lambda i, d_ref: (0, d_ref[0])),
                full((TOK, QD)),
            ],
            out_specs=[full((ROWS, WIDE))] * 2,
        ),
        out_shape=[shape, shape],
        compiler_params=params(MOST),
        cost_estimate=COST,
    )(d, hbm(ids), hbm(gates), hbm(tokens), hbm(cot))


def touch_kernel(_, out_ref):
    out_ref[...] = jnp.zeros_like(out_ref)


def touch_call(x):
    return pl.pallas_call(
        touch_kernel,
        in_specs=[pl.BlockSpec(memory_space=pl.ANY)],
        out_shape=jax.ShapeDtypeStruct((8, LANE), F32),
        compiler_params=params(),
        cost_estimate=COST,
    )(x)


def part_of(d, j):
    return pl.ds(pl.multiple_of(((d + j) % NDP) * QD, QD), QD)


NEAR = (0, 1, 3)
FAR = (2,)
IN_W = (QD, 2 * HD)
DOWN_W = (2 * HD, QD)


def fetch(d, pair, buf, sems, pieces, down, i):
    copies = []
    for c, w in enumerate(pair):
        own = pl.ds(c * HD, HD)
        if down:
            src, dst = w.at[:, part_of(d, pieces[i])], buf.at[i, own, :]
        else:
            src, dst = w.at[part_of(d, pieces[i]), :], buf.at[i, :, own]
        copies.append(pltpu.make_async_copy(src, dst, sems.at[i, c]))
        copies[-1].start()
    return copies


def bring(src, dst, sem):
    copy = pltpu.make_async_copy(src, dst, sem)
    copy.start()
    return copy


def wait_for(copies):
    for copy in copies:
        copy.wait()


def fetch_all(d, pair, buf, sems, pieces, down):
    return [fetch(d, pair, buf, sems, pieces, down, i) for i in range(len(pieces))]


def fwd_near_kernel(d_ref, own, high, low, wg0, wg1, wu0, wu1, sums, gate, up, gate_sem, up_sem):
    d = d_ref[0]
    weights = []
    for i in range(len(NEAR)):
        weights.append(fetch(d, (wg0, wg1), gate, gate_sem, NEAR, False, i))
        weights.append(fetch(d, (wu0, wu1), up, up_sem, NEAR, False, i))
    for i, piece in enumerate((own, high, low)):
        rows = join(piece[...])
        for k, buf in enumerate((gate, up)):
            wait_for(weights[2 * i + k])
            part = dot(rows, buf[i])
            sums[k] = part if i == 0 else sums[k] + part


def fwd_far_kernel(
    d_ref, far_a, far_b, wg0, wg1, wu0, wu1, wd0, wd1, sums, even,
    a_ref, b_ref, h_ref, out_a, out_b, gate, up, down, near, gate_sem, up_sem, down_sem, near_sem, in_sem,
):
    d = d_ref[0]
    gates = fetch(d, (wg0, wg1), gate, gate_sem, FAR, False, 0)
    ups = fetch(d, (wu0, wu1), up, up_sem, FAR, False, 0)
    a_copy = bring(sums.at[0], a_ref, in_sem.at[0])
    b_copy = bring(sums.at[1], b_ref, in_sem.at[1])
    downs = fetch(d, (wd0, wd1), down, down_sem, FAR, True, 0)
    nears = fetch_all(d, (wd0, wd1), near, near_sem, NEAR, True)
    rows = join(jnp.concatenate([far_a[...], far_b[...]], axis=0))
    wait_for(gates)
    part = dot(rows, gate[0])
    a_copy.wait()
    a_ref[...] = a_ref[...] + part
    wait_for(ups)
    part = dot(rows, up[0])
    b_copy.wait()
    b_ref[...] = b_ref[...] + part
    a, b = a_ref[...], b_ref[...]
    h_ref[...] = (a * jax.nn.sigmoid(a) * b).astype(BF)
    wait_for(downs)
    out = split(dot(h_ref[...], down[0]).astype(BF))
    out_a[...] = out[:HALF]
    out_b[...] = out[HALF:]
    for copies in nears:
        wait_for(copies)


def fwd_rest_kernel(d_ref, h_ref, down, wg0, wg1, own, high, low, gate, gate_sem):
    copies = fetch_all(d_ref[0], (wg0, wg1), gate, gate_sem, NEAR, False)
    for i, ref in enumerate((own, high, low)):
        ref[...] = split(dot(h_ref[...], down[i]).astype(BF))
    for copy in copies:
        wait_for(copy)


def bwd_near_kernel(d_ref, own, high, low, down, wu0, wu1, g_ref, up, up_sem):
    copies = fetch_all(d_ref[0], (wu0, wu1), up, up_sem, NEAR, False)
    for i, piece in enumerate((own, high, low)):
        part = dot(join(piece[...]), down[i], NT)
        g_ref[...] = part if i == 0 else g_ref[...] + part
    for copy in copies:
        wait_for(copy)


def bwd_far_kernel(d_ref, far_a, far_b, g_in, a_ref, b_ref, gate, up, down, da_ref, db_ref, out_a, out_b):
    rows = join(jnp.concatenate([far_a[...], far_b[...]], axis=0))
    g = g_in[...] + dot(rows, down[0], NT)
    a, b = a_ref[...], b_ref[...]
    s = jax.nn.sigmoid(a)
    da_ref[...] = (g * b * s * (1.0 + a * (1.0 - s))).astype(BF)
    db_ref[...] = (g * a * s).astype(BF)
    out = split((dot(da_ref[...], gate[0], NT) + dot(db_ref[...], up[0], NT)).astype(BF))
    out_a[...] = out[:HALF]
    out_b[...] = out[HALF:]


def bwd_rest_kernel(d_ref, da_ref, db_ref, gate, up, own, high, low):
    for i, ref in enumerate((own, high, low)):
        ref[...] = split((dot(da_ref[...], gate[i], NT) + dot(db_ref[...], up[i], NT)).astype(BF))


INSIDE = pl.BlockSpec(memory_space=pltpu.VMEM)
OUTSIDE = pl.BlockSpec(memory_space=pltpu.HBM)
HIDDEN = (ALL, 2 * HD)


def sems(*shape):
    return pltpu.SemaphoreType.DMA(shape)


def expert_call(kernel, d, inside, outside, outs, scratch=(), far_outs=()):
    return pl.pallas_call(
        kernel,
        in_specs=[pl.BlockSpec(memory_space=pltpu.SMEM)] + [INSIDE] * len(inside) + [OUTSIDE] * len(outside),
        out_specs=[INSIDE] * len(outs) + [OUTSIDE] * len(far_outs),
        out_shape=[jax.ShapeDtypeStruct(shape, kind) for shape, kind in (*outs, *far_outs)],
        scratch_shapes=list(scratch),
        compiler_params=params(),
        cost_estimate=COST if kernel in (fwd_far_kernel, fwd_rest_kernel, bwd_far_kernel) else LONG_COST,
    )(d, *inside, *outside)


def halves_kernel(high, low, low_a, high_b):
    low_a[...] = low[:HALF]
    high_b[...] = high[HALF:]


def halves_call(high, low):
    return local_call(halves_kernel, [HALF_ROWS] * 2, high, low)


SLOT_ROWS = ((ROWS, WIDE), BF)
HALF_ROWS = ((HALF, WIDE), BF)
SUMS = (HIDDEN, F32)
UNITS = (HIDDEN, BF)


def mix_kernel(ids_ref, gates_ref, cot_ref, out_ref, mixed_ref, dg_ref, hot_ref):
    hots = choose(ids_ref[...])
    hot_ref[...] = hots[0] + hots[1]
    rows = join(out_ref[...])
    gate = [col[:, :1] for col in columns(gates_ref[...])]
    cot = cot_ref[...].astype(F32)
    mixed = jnp.zeros((TOK, QD), F32)
    for k in range(2):
        mine = dot(hots[k], rows)
        mixed = mixed + gate[k] * mine
        dg_ref[:, k:k + 1] = jnp.sum(cot * mine, axis=1, keepdims=True)
    mixed_ref[...] = mixed.astype(BF)


def mix_call(ids, gates, cot, out):
    return pl.pallas_call(
        mix_kernel,
        out_shape=[
            jax.ShapeDtypeStruct((TOK, QD), BF),
            jax.ShapeDtypeStruct((TOK, 2), F32),
            jax.ShapeDtypeStruct((TOK, ALL), BF),
        ],
        compiler_params=params(),
        cost_estimate=COST,
    )(ids, gates, cot, out)


def dtok_kernel(hot_ref, dx_ref, out_ref):
    out_ref[...] = dot(hot_ref[...], join(dx_ref[...])).astype(BF)


def dtok_call(hot, dx):
    return pl.pallas_call(
        dtok_kernel,
        out_shape=jax.ShapeDtypeStruct((TOK, QD), BF),
        compiler_params=params(),
        cost_estimate=COST,
    )(hot, dx)


def move(x, by):
    return lax.ppermute(x, "dp", [(i, (i + by) % NDP) for i in range(NDP)])


def gather_near(own):
    return move(own, -1), move(own, 1)


def gather_far(high, low):
    low_a, high_b = halves_call(high, low)
    return move(low_a, 1), move(high_b, -1)


def local_call(kernel, outs, *ins):
    return pl.pallas_call(
        kernel,
        out_shape=[jax.ShapeDtypeStruct(shape, kind) for shape, kind in outs],
        compiler_params=params(),
        cost_estimate=COST,
    )(*ins)


def add(*terms):
    total = terms[0].astype(F32)
    for term in terms[1:]:
        total = total + term.astype(F32)
    return total.astype(BF)


def add_far_kernel(high, low, got_a, got_b, high_out, low_out):
    high_out[:HALF] = add(high[:HALF], got_a[...])
    high_out[HALF:] = high[HALF:]
    low_out[:HALF] = low[:HALF]
    low_out[HALF:] = add(low[HALF:], got_b[...])


def add_near_kernel(own, from_low, from_high, out):
    out[...] = add(own[...], from_low[...], from_high[...])


def reduce_far(far_a, far_b):
    return move(far_a, 1), move(far_b, -1)


def reduce_near(high, low, got_a, got_b):
    high, low = local_call(add_far_kernel, [SLOT_ROWS] * 2, high, low, got_a, got_b)
    return move(high, 1), move(low, -1)


def finish(own, from_low, from_high):
    return local_call(add_near_kernel, [SLOT_ROWS], own, from_low, from_high)[0]


def exchange(x):
    x = x.reshape(EXP, MAIN, WIDE)
    return lax.all_to_all(x, "expert", split_axis=0, concat_axis=0, tiled=True).reshape(ROWS, WIDE)


def after(x, *others):
    return lax.optimization_barrier((x, *others))[0]


def body(tokens, expert_ids, gates, w_gate, w_up, w_down, cotangent):
    d = lax.axis_index("dp").astype(jnp.int32).reshape(1)
    swap = lambda w: lax.ppermute(w, "group", [(0, 1), (1, 0)])
    wg, wu, wd = ((hbm(w[0]), hbm(swap(w[0]))) for w in (w_gate, w_up, w_down))
    ids, gates = expert_ids.T, gates.T
    x_pack, z_pack = pack_call(d, ids, gates, tokens, cotangent)
    x_own = exchange(x_pack)
    x_high, x_low = gather_near(x_own)
    z_own = exchange(after(z_pack, x_own))
    x_far = gather_far(x_high, x_low)
    even = lax.ppermute(touch_call(x_low), "group", [(0, 1), (1, 0)])
    (sums,) = expert_call(
        fwd_near_kernel, d, (x_own, x_high, x_low), (*wg, *wu), [((2, *HIDDEN), F32)],
        [pltpu.VMEM((3, *IN_W), BF)] * 2 + [sems(3, 2), sems(3, 2)],
    )
    z_own = after(z_own, sums, *x_far)
    z_high, z_low = gather_near(z_own)
    a, b, h, far_a, far_b, gate_far, up_far, down_far, down_near = expert_call(
        fwd_far_kernel, d, x_far, (*wg, *wu, *wd, hbm(sums), even),
        [SUMS, SUMS, UNITS, HALF_ROWS, HALF_ROWS, *(((1, *w), BF) for w in (IN_W, IN_W, DOWN_W)), ((3, *DOWN_W), BF)],
        [sems(1, 2), sems(1, 2), sems(1, 2), sems(3, 2), sems(2)],
    )
    got = reduce_far(far_a, far_b)
    out_own, out_high, out_low, gate_near = expert_call(
        fwd_rest_kernel, d, (h, down_near), wg, [SLOT_ROWS] * 3 + [((3, *IN_W), BF)], [sems(3, 2)]
    )
    z_far = gather_far(z_high, z_low)
    g, up_near = expert_call(
        bwd_near_kernel, d, (z_own, z_high, z_low, down_near), wu, [SUMS, ((3, *IN_W), BF)], [sems(3, 2)]
    )
    out_low = after(out_low, g)
    from_low, from_high = reduce_near(out_high, out_low, *got)
    da, db, far_a, far_b = expert_call(
        bwd_far_kernel, d, (*z_far, g, a, b, gate_far, up_far, down_far), (),
        [UNITS, UNITS, HALF_ROWS, HALF_ROWS],
    )
    got = reduce_far(far_a, far_b)
    dx_own, dx_high, dx_low = expert_call(
        bwd_rest_kernel, d, (da, db, gate_near, up_near), (), [SLOT_ROWS] * 3
    )
    out = exchange(after(finish(out_own, from_low, from_high), dx_own, *got))
    from_low, from_high = reduce_near(dx_high, dx_low, *got)
    dx = exchange(finish(dx_own, from_low, from_high))
    mixed, partial, hot = mix_call(ids, gates, cotangent, out)
    d_gates = (partial + move(partial, 2)) + (move(partial, 1) + move(partial, 3))
    d_tokens = dtok_call(hot, dx)
    return mixed, d_tokens, d_gates


def solution(mesh):
    in_specs = (
        P(("group", "expert"), None),
        P(("group", "expert"), None),
        P(("group", "expert"), None),
        P("expert", None, ("dp", "group")),
        P("expert", None, ("dp", "group")),
        P("expert", ("dp", "group"), None),
        P(("group", "expert"), "dp"),
    )
    out_specs = (
        P(("group", "expert"), "dp"),
        P(("group", "expert"), "dp"),
        P(("group", "expert"), None),
    )
    return jax.shard_map(body, mesh=mesh, in_specs=in_specs, out_specs=out_specs, check_vma=False)
```

```python
import functools
import jax
import jax.numpy as jnp
from jax import lax
from jax.experimental import pallas as pl
from jax.experimental.pallas import tpu as pltpu
from jax.sharding import PartitionSpec as P

BF = jnp.bfloat16
F32 = jnp.float32
TOK = 128
EXP = 32
MAIN = 8
OVER = 2
LANE = 128
NDP = 4
D = 3584
QD = D // NDP
CH = QD // LANE
ROWS = EXP * MAIN
WIDE = QD + OVER * LANE
ALL = ROWS + EXP * OVER
HALF = ROWS // 2
HD = 384
VMEM = 20 * 1024 * 1024
MOST = 56 * 1024 * 1024
COST = pl.CostEstimate(flops=1000, bytes_accessed=1000, transcendentals=0)
LONG_COST = pl.CostEstimate(flops=6_000_000_000, bytes_accessed=1000, transcendentals=0)
NT = (((1,), (1,)), ((), ()))
TN = (((0,), (0,)), ((), ()))


def hbm(x):
    return pltpu.with_memory_space_constraint(x, pltpu.HBM)


def params(limit=VMEM):
    return pltpu.CompilerParams(vmem_limit_bytes=limit)


def iota(shape, dim):
    return lax.broadcasted_iota(jnp.int32, shape, dim)


def dot(a, b, dims=(((1,), (0,)), ((), ()))):
    return lax.dot_general(a, b, dims, preferred_element_type=F32)


def spread(flip):
    shape = (CH * EXP, ROWS) if flip else (ROWS, CH * EXP)
    row, col = iota(shape, int(flip)), iota(shape, 1 - int(flip))
    return ((row % MAIN == col // EXP) & (row // MAIN == col % EXP)).astype(F32).astype(BF)


def pack(over):
    parts = [
        jnp.concatenate([over[c * EXP:(c + 1) * EXP, r * LANE:(r + 1) * LANE] for c in range(OVER)], axis=1)
        for r in range(CH)
    ]
    return dot(spread(False), jnp.concatenate(parts, axis=0)).astype(BF)


def unpack(packed):
    rows = dot(spread(True), packed).astype(BF)
    parts = [
        jnp.concatenate([rows[r * EXP:(r + 1) * EXP, c * LANE:(c + 1) * LANE] for c in range(OVER)], axis=0)
        for r in range(CH)
    ]
    return jnp.concatenate(parts, axis=1)


def join(piece):
    return jnp.concatenate([piece[:, :QD], unpack(piece[:, QD:])], axis=0)


def split(rows):
    return jnp.concatenate([rows[:ROWS], pack(rows[ROWS:])], axis=1)


def columns(rows):
    return [jnp.broadcast_to(rows[k:k + 1], (TOK, TOK)).T for k in range(2)]


def choose(ids):
    lane = iota((TOK, EXP), 1).astype(F32)
    cols = columns(ids.astype(F32))
    hot = [(col[:, :EXP] == lane).astype(F32) for col in cols]
    lower = (iota((TOK, TOK), 1) < iota((TOK, TOK), 0)).astype(F32).astype(BF)
    earlier = dot(lower, (hot[0] + hot[1]).astype(BF))
    out = []
    for k in range(2):
        slot = jnp.sum(earlier * hot[k], axis=1, keepdims=True)
        e = cols[k][:, :1]
        dest = jnp.where(slot < MAIN, e * MAIN + slot, ROWS + (slot - MAIN) * EXP + e).astype(jnp.int32)
        out.append((iota((TOK, ALL), 1) == dest).astype(F32).astype(BF))
    return out


def choose_rows(ids):
    lane = iota((EXP, TOK), 0)
    hot = [(lane == ids[k:k + 1]).astype(F32) for k in range(2)]
    upper = (iota((TOK, TOK), 0) < iota((TOK, TOK), 1)).astype(F32).astype(BF)
    earlier = dot((hot[0] + hot[1]).astype(BF), upper)
    out = []
    for k in range(2):
        slot = jnp.sum(earlier * hot[k], axis=0, keepdims=True).astype(jnp.int32)
        e = ids[k:k + 1]
        dest = jnp.where(slot < MAIN, e * MAIN + slot, ROWS + (slot - MAIN) * EXP + e)
        out.append((iota((ALL, TOK), 0) == dest).astype(F32))
    return out


def pack_kernel(d_ref, ids_ref, gates_ref, tok_ref, cot_ref, x_ref, z_ref):
    m0, m1 = choose_rows(ids_ref[...])
    gates = gates_ref[...]
    hot = (m0 + m1).astype(BF)
    x_ref[...] = split(dot(hot, tok_ref[...]).astype(BF))
    gate = jnp.sum(m0 * gates[0:1] + m1 * gates[1:2], axis=1, keepdims=True)
    z_ref[...] = split((gate * dot(hot, cot_ref[...])).astype(BF))


def pack_call(d, ids, gates, tokens, cot):
    full = lambda shape: pl.BlockSpec(shape, lambda i, d_ref: (0, 0))
    shape = jax.ShapeDtypeStruct((ROWS, WIDE), BF)
    return pl.pallas_call(
        pack_kernel,
        grid_spec=pltpu.PrefetchScalarGridSpec(
            num_scalar_prefetch=1,
            grid=(1,),
            in_specs=[
                full((2, TOK)),
                full((2, TOK)),
                pl.BlockSpec((TOK, QD), lambda i, d_ref: (0, d_ref[0])),
                full((TOK, QD)),
            ],
            out_specs=[full((ROWS, WIDE))] * 2,
        ),
        out_shape=[shape, shape],
        compiler_params=params(MOST),
        cost_estimate=COST,
    )(d, hbm(ids), hbm(gates), hbm(tokens), hbm(cot))


def touch_kernel(_, out_ref):
    out_ref[...] = jnp.zeros_like(out_ref)


def touch_call(x):
    return pl.pallas_call(
        touch_kernel,
        in_specs=[pl.BlockSpec(memory_space=pl.ANY)],
        out_shape=jax.ShapeDtypeStruct((8, LANE), F32),
        compiler_params=params(),
        cost_estimate=COST,
    )(x)


def part_of(d, j):
    return pl.ds(pl.multiple_of(((d + j) % NDP) * QD, QD), QD)


NEAR = (0, 1, 3)
FAR = (2,)
IN_W = (QD, 2 * HD)
DOWN_W = (2 * HD, QD)


def fetch(d, pair, buf, sems, pieces, down, i):
    copies = []
    for c, w in enumerate(pair):
        own = pl.ds(c * HD, HD)
        if down:
            src, dst = w.at[:, part_of(d, pieces[i])], buf.at[i, own, :]
        else:
            src, dst = w.at[part_of(d, pieces[i]), :], buf.at[i, :, own]
        copies.append(pltpu.make_async_copy(src, dst, sems.at[i, c]))
        copies[-1].start()
    return copies


def bring(src, dst, sem):
    copy = pltpu.make_async_copy(src, dst, sem)
    copy.start()
    return copy


def wait_for(copies):
    for copy in copies:
        copy.wait()


def fetch_all(d, pair, buf, sems, pieces, down):
    return [fetch(d, pair, buf, sems, pieces, down, i) for i in range(len(pieces))]


def fwd_near_kernel(d_ref, own, high, low, wg0, wg1, wu0, wu1, sums, gate, up, gate_sem, up_sem):
    d = d_ref[0]
    weights = []
    for i in range(len(NEAR)):
        weights.append(fetch(d, (wg0, wg1), gate, gate_sem, NEAR, False, i))
        weights.append(fetch(d, (wu0, wu1), up, up_sem, NEAR, False, i))
    for i, piece in enumerate((own, high, low)):
        rows = join(piece[...])
        for k, buf in enumerate((gate, up)):
            wait_for(weights[2 * i + k])
            part = dot(rows, buf[i])
            sums[k] = part if i == 0 else sums[k] + part


def fwd_far_kernel(
    d_ref, far_a, far_b, wg0, wg1, wu0, wu1, wd0, wd1, sums,
    a_ref, b_ref, h_ref, out_a, out_b, gate, up, down, near, gate_sem, up_sem, down_sem, near_sem, in_sem,
):
    d = d_ref[0]
    gates = fetch(d, (wg0, wg1), gate, gate_sem, FAR, False, 0)
    ups = fetch(d, (wu0, wu1), up, up_sem, FAR, False, 0)
    a_copy = bring(sums.at[0], a_ref, in_sem.at[0])
    b_copy = bring(sums.at[1], b_ref, in_sem.at[1])
    downs = fetch(d, (wd0, wd1), down, down_sem, FAR, True, 0)
    rows = join(jnp.concatenate([far_a[...], far_b[...]], axis=0))
    wait_for(gates)
    part = dot(rows, gate[0])
    a_copy.wait()
    a_ref[...] = a_ref[...] + part
    wait_for(ups)
    nears = fetch_all(d, (wd0, wd1), near, near_sem, NEAR, True)
    part = dot(rows, up[0])
    b_copy.wait()
    b_ref[...] = b_ref[...] + part
    a, b = a_ref[...], b_ref[...]
    h_ref[...] = (a * jax.nn.sigmoid(a) * b).astype(BF)
    wait_for(downs)
    out = split(dot(h_ref[...], down[0]).astype(BF))
    out_a[...] = out[:HALF]
    out_b[...] = out[HALF:]
    for copies in nears:
        wait_for(copies)


def fwd_rest_kernel(d_ref, h_ref, down, wg0, wg1, _, own, high, low, gate, gate_sem):
    copies = fetch_all(d_ref[0], (wg0, wg1), gate, gate_sem, NEAR, False)
    for i, ref in enumerate((own, high, low)):
        ref[...] = split(dot(h_ref[...], down[i]).astype(BF))
    for copy in copies:
        wait_for(copy)


def bwd_near_kernel(d_ref, own, high, low, down, wu0, wu1, g_ref, up, up_sem):
    copies = fetch_all(d_ref[0], (wu0, wu1), up, up_sem, NEAR, False)
    for i, piece in enumerate((own, high, low)):
        part = dot(join(piece[...]), down[i], NT)
        g_ref[...] = part if i == 0 else g_ref[...] + part
    for copy in copies:
        wait_for(copy)


def bwd_far_kernel(d_ref, far_a, far_b, g_in, a_ref, b_ref, gate, up, down, da_ref, db_ref, out_a, out_b):
    rows = join(jnp.concatenate([far_a[...], far_b[...]], axis=0))
    g = g_in[...] + dot(rows, down[0], NT)
    a, b = a_ref[...], b_ref[...]
    s = jax.nn.sigmoid(a)
    da_ref[...] = (g * b * s * (1.0 + a * (1.0 - s))).astype(BF)
    db_ref[...] = (g * a * s).astype(BF)
    out = split((dot(da_ref[...], gate[0], NT) + dot(db_ref[...], up[0], NT)).astype(BF))
    out_a[...] = out[:HALF]
    out_b[...] = out[HALF:]


def bwd_rest_kernel(d_ref, da_ref, db_ref, gate, up, own, high, low):
    for i, ref in enumerate((own, high, low)):
        ref[...] = split((dot(da_ref[...], gate[i], NT) + dot(db_ref[...], up[i], NT)).astype(BF))


INSIDE = pl.BlockSpec(memory_space=pltpu.VMEM)
OUTSIDE = pl.BlockSpec(memory_space=pltpu.HBM)
HIDDEN = (ALL, 2 * HD)


def sems(*shape):
    return pltpu.SemaphoreType.DMA(shape)


def expert_call(kernel, d, inside, outside, outs, scratch=(), far_outs=()):
    return pl.pallas_call(
        kernel,
        in_specs=[pl.BlockSpec(memory_space=pltpu.SMEM)] + [INSIDE] * len(inside) + [OUTSIDE] * len(outside),
        out_specs=[INSIDE] * len(outs) + [OUTSIDE] * len(far_outs),
        out_shape=[jax.ShapeDtypeStruct(shape, kind) for shape, kind in (*outs, *far_outs)],
        scratch_shapes=list(scratch),
        compiler_params=params(),
        cost_estimate=COST if kernel in (fwd_rest_kernel, bwd_far_kernel) else LONG_COST,
    )(d, *inside, *outside)


def halves_kernel(high, low, low_a, high_b):
    low_a[...] = low[:HALF]
    high_b[...] = high[HALF:]


def halves_call(high, low):
    return local_call(halves_kernel, [HALF_ROWS] * 2, high, low)


SLOT_ROWS = ((ROWS, WIDE), BF)
HALF_ROWS = ((HALF, WIDE), BF)
SUMS = (HIDDEN, F32)
UNITS = (HIDDEN, BF)


def mix_kernel(ids_ref, gates_ref, cot_ref, out_ref, mixed_ref, dg_ref, hot_ref):
    hots = choose(ids_ref[...])
    hot_ref[...] = hots[0] + hots[1]
    rows = join(out_ref[...])
    gate = [col[:, :1] for col in columns(gates_ref[...])]
    cot = cot_ref[...].astype(F32)
    mixed = jnp.zeros((TOK, QD), F32)
    for k in range(2):
        mine = dot(hots[k], rows)
        mixed = mixed + gate[k] * mine
        dg_ref[:, k:k + 1] = jnp.sum(cot * mine, axis=1, keepdims=True)
    mixed_ref[...] = mixed.astype(BF)


def mix_call(ids, gates, cot, out):
    return pl.pallas_call(
        mix_kernel,
        out_shape=[
            jax.ShapeDtypeStruct((TOK, QD), BF),
            jax.ShapeDtypeStruct((TOK, 2), F32),
            jax.ShapeDtypeStruct((TOK, ALL), BF),
        ],
        compiler_params=params(),
        cost_estimate=COST,
    )(ids, gates, cot, out)


def dtok_kernel(hot_ref, dx_ref, out_ref):
    out_ref[...] = dot(hot_ref[...], join(dx_ref[...])).astype(BF)


def dtok_call(hot, dx):
    return pl.pallas_call(
        dtok_kernel,
        out_shape=jax.ShapeDtypeStruct((TOK, QD), BF),
        compiler_params=params(),
        cost_estimate=COST,
    )(hot, dx)


def move(x, by):
    return lax.ppermute(x, "dp", [(i, (i + by) % NDP) for i in range(NDP)])


def gather_near(own):
    return move(own, -1), move(own, 1)


def gather_far(high, low):
    low_a, high_b = halves_call(high, low)
    return move(low_a, 1), move(high_b, -1)


def local_call(kernel, outs, *ins):
    return pl.pallas_call(
        kernel,
        out_shape=[jax.ShapeDtypeStruct(shape, kind) for shape, kind in outs],
        compiler_params=params(),
        cost_estimate=COST,
    )(*ins)


def add(*terms):
    total = terms[0].astype(F32)
    for term in terms[1:]:
        total = total + term.astype(F32)
    return total.astype(BF)


def add_far_kernel(high, low, got_a, got_b, high_out, low_out):
    high_out[:HALF] = add(high[:HALF], got_a[...])
    high_out[HALF:] = high[HALF:]
    low_out[:HALF] = low[:HALF]
    low_out[HALF:] = add(low[HALF:], got_b[...])


def add_near_kernel(own, from_low, from_high, out):
    out[...] = add(own[...], from_low[...], from_high[...])


def reduce_far(far_a, far_b):
    return move(far_a, 1), move(far_b, -1)


def reduce_near(high, low, got_a, got_b):
    high, low = local_call(add_far_kernel, [SLOT_ROWS] * 2, high, low, got_a, got_b)
    return move(high, 1), move(low, -1)


def finish(own, from_low, from_high):
    return local_call(add_near_kernel, [SLOT_ROWS], own, from_low, from_high)[0]


def exchange(x):
    x = x.reshape(EXP, MAIN, WIDE)
    return lax.all_to_all(x, "expert", split_axis=0, concat_axis=0, tiled=True).reshape(ROWS, WIDE)


def after(x, *others):
    return lax.optimization_barrier((x, *others))[0]


def body(tokens, expert_ids, gates, w_gate, w_up, w_down, cotangent):
    d = lax.axis_index("dp").astype(jnp.int32).reshape(1)
    swap = lambda w: lax.ppermute(w, "group", [(0, 1), (1, 0)])
    wg, wu, wd = ((hbm(w[0]), hbm(swap(w[0]))) for w in (w_gate, w_up, w_down))
    ids, gates = expert_ids.T, gates.T
    x_pack, z_pack = pack_call(d, ids, gates, tokens, cotangent)
    x_own = exchange(x_pack)
    x_high, x_low = gather_near(x_own)
    z_own = exchange(after(z_pack, x_own))
    x_far = gather_far(x_high, x_low)
    even = lax.ppermute(touch_call(x_low), "group", [(0, 1), (1, 0)])
    (sums,) = expert_call(
        fwd_near_kernel, d, (x_own, x_high, x_low), (*wg, *wu), [((2, *HIDDEN), F32)],
        [pltpu.VMEM((3, *IN_W), BF)] * 2 + [sems(3, 2), sems(3, 2)],
    )
    z_own = after(z_own, sums, *x_far)
    z_high, z_low = gather_near(z_own)
    a, b, h, far_a, far_b, gate_far, up_far, down_far, down_near = expert_call(
        fwd_far_kernel, d, x_far, (*wg, *wu, *wd, hbm(sums)),
        [SUMS, SUMS, UNITS, HALF_ROWS, HALF_ROWS, *(((1, *w), BF) for w in (IN_W, IN_W, DOWN_W)), ((3, *DOWN_W), BF)],
        [sems(1, 2), sems(1, 2), sems(1, 2), sems(3, 2), sems(2)],
    )
    got = reduce_far(far_a, far_b)
    out_own, out_high, out_low, gate_near = expert_call(
        fwd_rest_kernel, d, (h, down_near), (*wg, even), [SLOT_ROWS] * 3 + [((3, *IN_W), BF)], [sems(3, 2)]
    )
    z_far = gather_far(z_high, z_low)
    g, up_near = expert_call(
        bwd_near_kernel, d, (z_own, z_high, z_low, down_near), wu, [SUMS, ((3, *IN_W), BF)], [sems(3, 2)]
    )
    out_low = after(out_low, g)
    from_low, from_high = reduce_near(out_high, out_low, *got)
    da, db, far_a, far_b = expert_call(
        bwd_far_kernel, d, (*z_far, g, a, b, gate_far, up_far, down_far), (),
        [UNITS, UNITS, HALF_ROWS, HALF_ROWS],
    )
    got = reduce_far(far_a, far_b)
    dx_own, dx_high, dx_low = expert_call(
        bwd_rest_kernel, d, (da, db, gate_near, up_near), (), [SLOT_ROWS] * 3
    )
    out = exchange(after(finish(out_own, from_low, from_high), dx_own, *got))
    from_low, from_high = reduce_near(dx_high, dx_low, *got)
    dx = exchange(finish(dx_own, from_low, from_high))
    mixed, partial, hot = mix_call(ids, gates, cotangent, out)
    d_gates = (partial + move(partial, 2)) + (move(partial, 1) + move(partial, 3))
    d_tokens = dtok_call(hot, dx)
    return mixed, d_tokens, d_gates


def solution(mesh):
    in_specs = (
        P(("group", "expert"), None),
        P(("group", "expert"), None),
        P(("group", "expert"), None),
        P("expert", None, ("dp", "group")),
        P("expert", None, ("dp", "group")),
        P("expert", ("dp", "group"), None),
        P(("group", "expert"), "dp"),
    )
    out_specs = (
        P(("group", "expert"), "dp"),
        P(("group", "expert"), "dp"),
        P(("group", "expert"), None),
    )
    return jax.shard_map(body, mesh=mesh, in_specs=in_specs, out_specs=out_specs, check_vma=False)
```
